256 devices in a mesh: section: 4 (over x_lo, core), ctx: 16 (over z, x_hi), tp: 4 (over y).
Axes of the slice: x: 4 (x_hi: 2, x_lo: 2; x = x_hi * 2 + x_lo), y: 4, z: 8, core: 2. Of those that a mesh axis runs over, the one named last changes fastest.
Arguments:
- in_weights: bfloat16 [4, 3, 4096, 4096], P('section', None, 'ctx', 'tp'), may hold values from -0.09375 to 0.09375
- short_taps: float32 [4, 3, 7, 4096], P('section', None, None, 'tp'), may hold values from -2 to 2
- long_taps: float32 [4, 128, 4096], P('section', None, 'tp'), may hold values from -0.5 to 0.5
- first_saved: bfloat16 [4, 3, 4096, 4096], P('section', None, 'ctx', 'tp'), may hold values from -6 to 6
- second_saved: bfloat16 [4, 3, 4096, 4096], P('section', None, 'ctx', 'tp'), may hold values from -6 to 6
- first_cotangent: bfloat16 [4, 4096, 4096], P('section', 'ctx', 'tp'), may hold values from -6 to 6
- last_cotangent: bfloat16 [4096, 4096], P('ctx', 'tp'), may hold values from -6 to 6
Outputs:
- first_sent: bfloat16 [4, 4096, 4096], P('section', 'ctx', 'tp')
- second_sent: bfloat16 [4, 4096, 4096], P('section', 'ctx', 'tp')
The draws below stay inside these ranges and needn't reach their ends.
All inputs are finite; a program needn't handle non-finite values.
Results may differ from the reference program's by a relative error of at most 0.025.
Values may be sent and summed in bfloat16 or wider, within the bound.
A program may use at most 128 MiB of HBM per device.

```python
import jax
import jax.numpy as jnp
from jax import lax

D = 4096
SHORT = 7
FILT = 128
TOKENS = 4096
N_SECTION = 4
N_TP = 4


def block_levels(key, shape, shards, low, high):
    def one(dim, parts):
        steps = jax.random.uniform(jax.random.fold_in(jax.random.fold_in(key, 6), dim), (parts,), jnp.float32, low / len(shards), high / len(shards))
        return jnp.repeat(jnp.exp(steps), shape[dim] // parts).reshape((-1,) + (1,) * (len(shape) - dim - 1))

    loudness = one(*shards[0])
    for cut in shards[1:]:
        loudness = loudness * one(*cut)
    return loudness


def noise(rng, extent, scale, reach, split=(), kind=jnp.bfloat16):
    array = scale * jax.random.normal(rng, extent, jnp.float32)
    if split:
        array = array * block_levels(rng, extent, split, -0.22, 0.18)
    return jnp.clip(array, -reach, reach).astype(kind)


def setup_inputs(seed: int = 0) -> dict:
    key_of = jax.random.split(jax.random.key(seed), 8)
    in_weights = noise(key_of[0], (N_SECTION, 3, D, D), D ** -0.5, 0.09375, ((0, 4), (2, 16), (3, 4)))
    short_taps = noise(key_of[1], (N_SECTION, 3, SHORT, D), SHORT ** -0.5, 2.0, ((0, 4), (3, 4)), jnp.float32)
    long_taps = noise(key_of[2], (N_SECTION, FILT, D), FILT ** -0.5, 0.5, ((0, 4), (2, 4)), jnp.float32)
    first_saved = noise(key_of[3], (N_SECTION, 3, TOKENS, D), 1.0, 6.0, ((0, 4), (2, 16), (3, 4)))
    second_saved = noise(key_of[4], (N_SECTION, 3, TOKENS, D), 1.0, 6.0, ((0, 4), (2, 16), (3, 4)))
    first_cotangent = noise(key_of[5], (N_SECTION, TOKENS, D), 1.0, 6.0, ((0, 4), (1, 16), (2, 4)))
    last_cotangent = noise(key_of[6], (TOKENS, D), 1.0, 6.0, ((0, 16), (1, 4)))
    return {"in_weights": in_weights, "short_taps": short_taps, "long_taps": long_taps, "first_saved": first_saved, "second_saved": second_saved, "first_cotangent": first_cotangent, "last_cotangent": last_cotangent}


def depthwise(padded, kernel):
    width = kernel.shape[0]
    length = padded.shape[0] - width + 1

    def add_tap(index, total):
        rows = lax.dynamic_slice_in_dim(padded, index, length, 0)
        return total + rows * lax.dynamic_index_in_dim(kernel, index, 0, keepdims=True)

    start = jnp.zeros((length, padded.shape[1]), padded.dtype)
    return lax.fori_loop(0, width, add_tap, start)


def causal(signal, filter_taps):
    width = filter_taps.shape[0]
    padded = jnp.pad(signal, ((width - 1, 0), (0, 0)))
    return depthwise(padded, filter_taps[::-1])


def anticausal(signal, filter_taps):
    width = filter_taps.shape[0]
    padded = jnp.pad(signal, ((0, width - 1), (0, 0)))
    return depthwise(padded, filter_taps)


def section_backward(weights, short_filter, long_filter, saved, cotangent):
    inputs = saved.astype(jnp.float32)
    features = [causal(inputs[member], short_filter[member]) for member in range(3)]
    product = features[1] * features[2]
    mixed = causal(product, long_filter)
    upstream = cotangent.astype(jnp.float32)
    dquery = upstream * mixed
    dmixed = upstream * features[0]
    dproduct = anticausal(dmixed, long_filter)
    dfeatures = [dquery, dproduct * features[2], dproduct * features[1]]
    dinputs = jnp.stack([anticausal(dfeatures[member], short_filter[member]) for member in range(3)]).astype(jnp.bfloat16)
    length = dinputs.shape[1]
    block = D // N_TP
    total = jnp.zeros((length, D), jnp.float32)
    for block_id in range(N_TP):
        left = jnp.transpose(dinputs[:, :, block_id * block:(block_id + 1) * block], (1, 0, 2)).reshape(length, 3 * block)
        right = jnp.transpose(weights[:, :, block_id * block:(block_id + 1) * block], (1, 0, 2)).reshape(D, 3 * block)
        partial_sum = jnp.dot(left, right.T, preferred_element_type=jnp.float32)
        total = total + lax.optimization_barrier(partial_sum.astype(jnp.bfloat16)).astype(jnp.float32)
    return (upstream + total).astype(jnp.bfloat16)


def reference(in_weights, short_taps, long_taps, first_saved, second_saved, first_cotangent, last_cotangent):
    first_list = [section_backward(in_weights[section_id], short_taps[section_id], long_taps[section_id], first_saved[section_id], first_cotangent[section_id]) for section_id in range(N_SECTION)]
    second_list = []
    for section_id in range(N_SECTION):
        incoming = first_list[section_id + 1] if section_id + 1 < N_SECTION else last_cotangent
        second_list.append(section_backward(in_weights[section_id], short_taps[section_id], long_taps[section_id], second_saved[section_id], incoming))
    return jnp.stack(first_list), jnp.stack(second_list)
```

```python
import numpy as np
import jax
import jax.numpy as jnp
from jax import lax
from jax.sharding import PartitionSpec as P

N = 256
HALF = 128


def shifted_dft():
    k = np.arange(HALF)[:, None] + 0.5
    n = np.arange(N)[None, :]
    angle = 2.0 * np.pi * k * n / N
    forward = np.concatenate([np.cos(angle), -np.sin(angle)], axis=0)
    inverse = np.concatenate([np.cos(angle), -np.sin(angle)], axis=0).T * (2.0 / N)
    return forward.astype(np.float32), inverse.astype(np.float32)


FORWARD, INVERSE = shifted_dft()


def passed_along(block, axis, distance):
    devices = range(lax.axis_size(axis))
    route = [(i - distance, i) for i in devices if i - distance in devices]
    return lax.ppermute(block, axis, route)


def dot(a, b):
    return jnp.dot(a.astype(jnp.bfloat16), b.astype(jnp.bfloat16), preferred_element_type=jnp.float32)


def long_filter(signal, response, causal):
    real, imag = response
    pieces = []
    for start in range(0, signal.shape[0] - HALF, HALF):
        spectrum = dot(FORWARD, signal[start : start + N])
        a, b = spectrum[:HALF], spectrum[HALF:]
        if causal:
            mixed = jnp.concatenate([a * real - b * imag, a * imag + b * real], axis=0)
            pieces.append(dot(INVERSE[HALF:], mixed))
        else:
            mixed = jnp.concatenate([a * real + b * imag, b * real - a * imag], axis=0)
            pieces.append(dot(INVERSE[:HALF], mixed))
    return jnp.concatenate(pieces, axis=0)


def short_causal(padded, taps):
    length = padded.shape[0] - 6
    return sum(padded[6 - i : 6 - i + length] * taps[i][None, :] for i in range(7))


def short_anticausal(padded, taps):
    length = padded.shape[0] - 6
    return sum(padded[i : i + length] * taps[i][None, :] for i in range(7))


def slot_backward(weight_block, short_filter, response, saved, cotangent):
    length = saved.shape[1]
    before_rows = passed_along(saved[:, length - 6 :, :], "ctx", 1)
    inputs = jnp.concatenate([before_rows, saved], axis=1).astype(jnp.float32)
    features = [short_causal(inputs[member], short_filter[member]) for member in range(3)]
    product = features[1] * features[2]
    prior_rows = passed_along(product[length - HALF :].astype(jnp.bfloat16), "ctx", 1)
    mixed = long_filter(
        jnp.concatenate([prior_rows, product.astype(jnp.bfloat16)], axis=0), response, True
    )
    upstream = cotangent.astype(jnp.float32)
    dquery = upstream * mixed
    dmixed = (upstream * features[0]).astype(jnp.bfloat16)
    after_rows = passed_along(dmixed[:HALF], "ctx", -1)
    dproduct = long_filter(jnp.concatenate([dmixed, after_rows], axis=0), response, False)
    dfeatures = jnp.stack([dquery, dproduct * features[2], dproduct * features[1]])
    following = passed_along(dfeatures[:, :6, :].astype(jnp.bfloat16), "ctx", -1)
    extended = jnp.concatenate([dfeatures, following.astype(jnp.float32)], axis=1)
    dinputs = jnp.stack(
        [short_anticausal(extended[member], short_filter[member]) for member in range(3)]
    ).astype(jnp.bfloat16)
    term = jnp.einsum("jtc,jmc->tm", dinputs, weight_block, preferred_element_type=jnp.float32)
    summed = lax.psum_scatter(
        term.astype(jnp.bfloat16), "tp", scatter_dimension=1, tiled=True
    ).astype(jnp.float32)
    return (upstream + summed).astype(jnp.bfloat16)


def body(
    in_weights, short_taps, long_taps, first_saved, second_saved, first_cotangent, last_cotangent
):
    weight_block = lax.all_gather(in_weights[0], "ctx", axis=1, tiled=True)
    spectrum = jnp.dot(FORWARD[:, :HALF], long_taps[0], precision=lax.Precision.HIGHEST)
    response = (spectrum[:HALF], spectrum[HALF:])
    first_result = slot_backward(
        weight_block, short_taps[0], response, first_saved[0], first_cotangent[0]
    )
    arrived = passed_along(first_result, "section", -1)
    is_final = lax.axis_index("section") == lax.axis_size("section") - 1
    incoming = jnp.where(is_final, last_cotangent, arrived)
    second_result = slot_backward(
        weight_block, short_taps[0], response, second_saved[0], incoming
    )
    return (first_result[None], second_result[None])


def solution(mesh):
    in_specs = (
        P("section", None, "ctx", "tp"),
        P("section", None, None, "tp"),
        P("section", None, "tp"),
        P("section", None, "ctx", "tp"),
        P("section", None, "ctx", "tp"),
        P("section", "ctx", "tp"),
        P("ctx", "tp"),
    )
    out_specs = (P("section", "ctx", "tp"), P("section", "ctx", "tp"))
    return jax.shard_map(body, mesh=mesh, in_specs=in_specs, out_specs=out_specs, check_vma=False)
```

```python
import functools

import numpy as np
import jax
import jax.numpy as jnp
from jax import lax
from jax.experimental import pallas as pl
from jax.experimental.pallas import tpu as pltpu
from jax.sharding import PartitionSpec as P

MESH = pl.DeviceIdType.MESH
N = 256
HALF = 128
BEFORE = 144
AFTER = 160
GROUP = 512
ROWS = BEFORE + GROUP + AFTER
REACH = GROUP + AFTER
KEPT = GROUP + 16
CHUNK = 256
TILE = 32
f32 = jnp.float32
bf16 = jnp.bfloat16


def shifted_dft():
    k = np.arange(HALF)[:, None] + 0.5
    n = np.arange(N)[None, :]
    angle = 2.0 * np.pi * k * n / N
    forward = np.concatenate([np.cos(angle), -np.sin(angle)], axis=0)
    return forward.astype(np.float32), (forward.T * (2.0 / N)).astype(np.float32)


FORWARD, INVERSE = shifted_dft()


def dot(a, b):
    return jnp.dot(a, b, preferred_element_type=f32)


def filtered(forward, inverse, signal, real, imag):
    spectrum = dot(forward, signal)
    a, b = spectrum[:HALF], spectrum[HALF:]
    mixed = jnp.concatenate([a * real - b * imag, a * imag + b * real], axis=0).astype(bf16)
    return dot(inverse, mixed)


def kernel(
    w_ref, short_ref, long_ref, u1_ref, u2_ref, g1_ref, gl_ref, fwd_ref, inv_ref, fwd32_ref,
    out1_ref, out2_ref,
    wb, ue, ge, p0, p1, p2, mx, di, pb, rb, sb, resp, pr, dm, df,
    ring_s, ring_r, x_s, x_r, loc, halo_s, halo_r, tp_s, tp_r, main_s, main_r, edge_s, edge_r,
    fin_s, fin_r,
):
    s = lax.axis_index("section")
    c = lax.axis_index("ctx")
    k = lax.axis_index("tp")
    z, h = c // 2, c % 2
    up, down = (z + 1) % 8, (z + 7) % 8
    partner = 2 * z + 1 - h
    last = s == 3

    def remote(src, dst, send, recv, device):
        return pltpu.make_async_remote_copy(
            src_ref=src, dst_ref=dst, send_sem=send, recv_sem=recv,
            device_id=device, device_id_type=MESH,
        )

    barrier = pltpu.get_barrier_semaphore()

    def greet(device):
        pl.semaphore_signal(barrier, inc=1, device_id=device, device_id_type=MESH)

    greet({"ctx": partner})
    for zz in (up, down):
        for hh in range(2):
            greet({"ctx": 2 * zz + hh})
    for step in range(1, 4):
        greet({"tp": (k + step) % 4})

    @pl.when(s < 3)
    def _():
        for zz in (z, up):
            for hh in range(2):
                greet({"section": s + 1, "ctx": 2 * zz + hh})

    pl.semaphore_wait(barrier, 8 + 4 * ((s + 3) // 4))

    def ring(j, to_right):
        target = {"ctx": 2 * (up if to_right else down) + h}
        after = j + 1 if to_right else (7 if j == 0 else j - 1)
        sem = j if to_right else 4 + (8 - j) % 8
        src, dst = (w_ref if j == 0 else wb.at[j]), wb.at[after]
        if after == 4:
            part = pl.ds(0 if to_right else 128, 128)
            src, dst = wb.at[j, :, part], wb.at[4, :, part]
        return remote(src, dst, ring_s.at[sem], ring_r.at[sem], target)

    rights = [ring(j, True) for j in (0, 1, 2, 3)]
    lefts = [ring(j, False) for j in (0, 7, 6, 5)]
    rights[0].start()
    lefts[0].start()

    own_rows = pl.ds(pl.multiple_of(BEFORE + 256 * h, 16), 256)
    other_rows = pl.ds(pl.multiple_of(BEFORE + 256 * (1 - h), 16), 256)
    own_g = pl.ds(pl.multiple_of(256 * h, 256), 256)
    other_g = pl.ds(pl.multiple_of(256 * (1 - h), 256), 256)
    saved = (u1_ref, u2_ref)
    grads = (g1_ref, gl_ref)

    local_w = pltpu.make_async_copy(w_ref, wb.at[0], loc.at[0])
    local_u = [pltpu.make_async_copy(saved[i], ue.at[i, :, own_rows], loc.at[1 + i]) for i in range(2)]
    local_g = [pltpu.make_async_copy(grads[i], ge.at[i, own_g], loc.at[3 + i]) for i in range(2)]
    send_u = [
        remote(saved[i], ue.at[i, :, own_rows], x_s.at[i], x_r.at[i], {"ctx": partner}) for i in range(2)
    ]
    send_g = [
        remote(grads[i], ge.at[i, own_g], x_s.at[2 + i], x_r.at[2 + i], {"ctx": partner})
        for i in range(2)
    ]
    get_u = [
        remote(saved[i], ue.at[i, :, other_rows], x_s.at[i], x_r.at[i], {"ctx": partner}) for i in range(2)
    ]
    get_g = [
        remote(grads[i], ge.at[i, other_g], x_s.at[2 + i], x_r.at[2 + i], {"ctx": partner})
        for i in range(2)
    ]

    def halo_before(i, hh):
        to = {"ctx": 2 * up + hh}
        u = saved[i]
        return [
            remote(u.at[pl.ds(1, 2), pl.ds(256 - BEFORE, BEFORE)], ue.at[i, pl.ds(1, 2), pl.ds(0, BEFORE)],
                   halo_s.at[i, 0, hh], halo_r.at[i, 0], to),
            remote(u.at[0, pl.ds(240, 16)], ue.at[i, 0, pl.ds(BEFORE - 16, 16)],
                   halo_s.at[i, 1, hh], halo_r.at[i, 1], to),
        ]

    def halo_after(i, hh):
        to = {"ctx": 2 * down + hh}
        u = saved[i]
        return [
            remote(u.at[0, pl.ds(0, AFTER)], ue.at[i, 0, pl.ds(BEFORE + GROUP, AFTER)],
                   halo_s.at[i, 0, hh], halo_r.at[i, 2], to),
            remote(u.at[pl.ds(1, 2), pl.ds(0, 32)], ue.at[i, pl.ds(1, 2), pl.ds(BEFORE + GROUP, 32)],
                   halo_s.at[i, 1, hh], halo_r.at[i, 3], to),
        ]

    def halo_g(i, hh):
        return remote(grads[i].at[pl.ds(0, AFTER)], ge.at[i, pl.ds(GROUP, AFTER)],
                      halo_s.at[i, 2, hh], halo_r.at[i, 4], {"ctx": 2 * down + hh})

    def start_halos(i):
        @pl.when(h == 1)
        def _():
            for hh in range(2):
                for copy in halo_before(i, hh):
                    copy.start()

        @pl.when(h == 0)
        def _():
            for hh in range(2):
                for copy in halo_after(i, hh):
                    copy.start()

    def end_halos(i):
        @pl.when(h == 1)
        def _():
            for hh in range(2):
                for copy in halo_before(i, hh):
                    copy.wait_send()

        @pl.when(h == 0)
        def _():
            for hh in range(2):
                for copy in halo_after(i, hh):
                    copy.wait_send()

    def receive_halos(i):
        for copy in halo_before(i, 0) + halo_after(i, 0):
            copy.wait_recv()

        @pl.when(z == 0)
        def _():
            ue[i, pl.ds(0, 3), pl.ds(BEFORE - 16, 16)] = jnp.zeros((3, 16, 1024), bf16)
            ue[i, pl.ds(1, 2), pl.ds(0, BEFORE - 16)] = jnp.zeros((2, BEFORE - 16, 1024), bf16)

    def clear_edge(i):
        @pl.when(z == 7)
        def _():
            ge[i, pl.ds(GROUP, AFTER)] = jnp.zeros((AFTER, 1024), bf16)

    local_u[0].start()
    local_g[0].start()
    send_u[0].start()
    send_g[0].start()
    start_halos(0)

    @pl.when(h == 0)
    def _():
        for hh in range(2):
            halo_g(0, hh).start()

    local_w.start()
    local_u[1].start()
    send_u[1].start()
    start_halos(1)

    @pl.when(last)
    def _():
        local_g[1].start()
        send_g[1].start()

        @pl.when(h == 0)
        def _():
            for hh in range(2):
                halo_g(1, hh).start()

    resp[...] = jnp.dot(
        fwd32_ref[...], long_ref[...], precision=lax.Precision.HIGHEST, preferred_element_type=f32
    )

    def columns(r):
        return pl.ds(pl.multiple_of(r * CHUNK, CHUNK), CHUNK)

    def features(i):
        def chunk(r, _):
            cols = columns(r)

            def short(m, x):
                total = x[16:] * short_ref[m, 0:1, cols]
                for tap in range(1, 7):
                    total += pltpu.roll(x, tap, 0)[16:] * short_ref[m, tap : tap + 1, cols]
                return total

            def tile(b, _):
                here = pl.ds(pl.multiple_of(b * TILE, TILE), TILE)
                wide = pl.ds(pl.multiple_of(b * TILE, TILE), TILE + 16)
                key = short(1, ue[i, 1, wide, cols].astype(f32))
                value = short(2, ue[i, 2, wide, cols].astype(f32))
                p1[here, cols] = key
                p2[here, cols] = value
                pr[here] = (key * value).astype(bf16)
                wide = pl.ds(pl.multiple_of(BEFORE - 16 + b * TILE, 16), TILE + 16)
                p0[here, cols] = short(0, ue[i, 0, wide, cols].astype(f32))
                return 0

            lax.fori_loop(0, REACH // TILE, tile, 0)
            real, imag = resp[:HALF, cols], resp[HALF:, cols]
            for b in range(4):
                mx[HALF * b : HALF * (b + 1), cols] = filtered(
                    fwd_ref[...], inv_ref[HALF:], pr[HALF * b : HALF * b + N], real, imag
                )
            mx[GROUP:KEPT, cols] = filtered(
                fwd_ref[:, :AFTER], inv_ref[HALF : HALF + 16], pr[GROUP:REACH], real, imag
            )
            return 0

        lax.fori_loop(0, 4, chunk, 0)

    def gradients(i):
        def chunk(r, _):
            cols = columns(r)

            def scale(b, _):
                here = pl.ds(pl.multiple_of(b * TILE, TILE), TILE)
                dm[here] = (ge[i, here, cols].astype(f32) * p0[here, cols]).astype(bf16)
                return 0

            lax.fori_loop(0, REACH // TILE, scale, 0)
            real, imag = resp[:HALF, cols], -resp[HALF:, cols]
            for b in range(5):
                rows = HALF if b < 4 else 16
                span = N if b < 4 else AFTER
                begin = HALF * b
                dproduct = filtered(
                    fwd_ref[:, :span], inv_ref[:rows], dm[begin : begin + span], real, imag
                )
                there = slice(begin, begin + rows)
                shifted = slice(begin + HALF, begin + HALF + rows)
                df[0, there] = ge[i, there, cols].astype(f32) * mx[there, cols]
                df[1, there] = dproduct * p2[shifted, cols]
                df[2, there] = dproduct * p1[shifted, cols]

            def tile(b, _):
                here = pl.ds(pl.multiple_of(b * TILE, TILE), TILE)
                wide = pl.ds(pl.multiple_of(b * TILE, TILE), TILE + 8)
                for m in range(3):
                    x = df[m, wide]
                    total = x[:TILE] * short_ref[m, 0:1, cols]
                    for tap in range(1, 7):
                        total += pltpu.roll(x, TILE + 8 - tap, 0)[:TILE] * short_ref[m, tap : tap + 1, cols]
                    di[m, here, cols] = total.astype(bf16)
                return 0

            lax.fori_loop(0, GROUP // TILE, tile, 0)
            return 0

        lax.fori_loop(0, 4, chunk, 0)

    def place(j):
        zt = (z + 8 - j) % 8
        return zt // 2, zt % 2

    def tp_copy(i, j):
        kt, q = place(j)
        return remote(pb.at[j], rb.at[i, k, q], tp_s.at[i, j], tp_r.at[i, k, q], {"tp": kt})

    def end_tp(i, j):
        kt, _ = place(j)

        @pl.when(kt != k)
        def _():
            tp_copy(i, j).wait_send()

    def multiply(i, lo, hi):
        def unit(n, _):
            odd = n % 2
            j = odd * ((n + 1) // 2) + (1 - odd) * ((8 - n // 2) % 8)
            if i == 1:
                end_tp(0, j)
            total = None
            for m in range(3):
                term = lax.dot_general(
                    di[m], wb[j, m], (((1,), (1,)), ((), ())), preferred_element_type=f32
                )
                total = term if total is None else total + term
            pb[j] = total.astype(bf16)
            kt, _q = place(j)

            @pl.when(kt != k)
            def _():
                tp_copy(i, j).start()

            return 0

        lax.fori_loop(lo, hi, unit, 0)

    def combine(i):
        for q in range(2):
            cols = columns(h + 2 * q)
            for step in range(1, 4):
                src = (k + step) % 4
                remote(pb.at[0], rb.at[i, src, q], tp_s.at[i, 0], tp_r.at[i, src, q], {"tp": src}).wait_recv()
            mine = (z + 8 - 2 * k - q) % 8

            def tile(b, _):
                here = pl.ds(pl.multiple_of(b * 64, 64), 64)
                total = ge[i, here, cols].astype(f32) + pb[mine, here].astype(f32)
                for step in range(1, 4):
                    total += rb[i, (k + step) % 4, q, here].astype(f32)
                sb[i, q, here] = total.astype(bf16)
                return 0

            lax.fori_loop(0, GROUP // 64, tile, 0)

    outs = (out1_ref, out2_ref)

    def finals(i, q):
        mine, theirs = columns(h + 2 * q), columns(1 - h + 2 * q)
        keep = pltpu.make_async_copy(sb.at[i, q, own_g], outs[i].at[:, mine], loc.at[5 + 2 * i + q])
        give = remote(sb.at[i, q, other_g], outs[i].at[:, mine], fin_s.at[i, q], fin_r.at[i, q], {"ctx": partner})
        take = remote(sb.at[i, q, other_g], outs[i].at[:, theirs], fin_s.at[i, q], fin_r.at[i, q], {"ctx": partner})
        return keep, give, take

    def relay(q, hh):
        r = h + 2 * q
        to = {"section": lax.rem(s + 3, 4), "ctx": 2 * z + hh}
        edge_to = {"section": lax.rem(s + 3, 4), "ctx": 2 * down + hh}
        return (
            remote(sb.at[0, q], ge.at[1, pl.ds(0, GROUP), columns(r)], main_s.at[q, hh], main_r.at[r], to),
            remote(sb.at[0, q, pl.ds(0, AFTER)], ge.at[1, pl.ds(GROUP, AFTER), columns(r)],
                   edge_s.at[q, hh], edge_r.at[r], edge_to),
        )

    rights[0].wait_recv()
    rights[1].start()
    lefts[0].wait_recv()
    lefts[1].start()
    local_u[0].wait()
    local_g[0].wait()
    get_u[0].wait_recv()
    receive_halos(0)
    features(0)
    rights[1].wait_recv()
    rights[2].start()
    lefts[1].wait_recv()
    lefts[2].start()
    get_g[0].wait_recv()
    halo_g(0, 0).wait_recv()
    clear_edge(0)
    gradients(0)
    local_u[1].wait()
    get_u[1].wait_recv()
    receive_halos(1)
    features(1)
    local_w.wait()
    multiply(0, 0, 5)
    rights[2].wait_recv()
    rights[3].start()
    lefts[2].wait_recv()
    lefts[3].start()
    multiply(0, 5, 7)
    rights[3].wait_recv()
    lefts[3].wait_recv()
    multiply(0, 7, 8)
    combine(0)

    @pl.when(s > 0)
    def _():
        for q in range(2):
            for hh in range(2):
                for copy in relay(q, hh):
                    copy.start()

    for q in range(2):
        keep, give, _ = finals(0, q)
        keep.start()
        give.start()

    @pl.when(last)
    def _():
        local_g[1].wait()
        get_g[1].wait_recv()
        halo_g(1, 0).wait_recv()

    @pl.when(s < 3)
    def _():
        for r in range(4):
            remote(sb.at[0, 0], ge.at[1, pl.ds(0, GROUP), columns(r)], main_s.at[0, 0], main_r.at[r],
                   {"ctx": partner}).wait_recv()
            remote(sb.at[0, 0, pl.ds(0, AFTER)], ge.at[1, pl.ds(GROUP, AFTER), columns(r)], edge_s.at[0, 0],
                   edge_r.at[r], {"ctx": partner}).wait_recv()

    clear_edge(1)
    gradients(1)
    multiply(1, 0, 8)
    combine(1)
    for q in range(2):
        keep, give, _ = finals(1, q)
        keep.start()
        give.start()

    for copy in rights + lefts:
        copy.wait_send()
    for i in range(2):
        send_u[i].wait_send()
        end_halos(i)
    send_g[0].wait_send()

    @pl.when(h == 0)
    def _():
        for hh in range(2):
            halo_g(0, hh).wait_send()

    @pl.when(last)
    def _():
        send_g[1].wait_send()

        @pl.when(h == 0)
        def _():
            for hh in range(2):
                halo_g(1, hh).wait_send()

    @pl.when(s > 0)
    def _():
        for q in range(2):
            for hh in range(2):
                for copy in relay(q, hh):
                    copy.wait_send()

    def finish(j, _):
        end_tp(1, j)
        return 0

    lax.fori_loop(0, 8, finish, 0)
    for i in range(2):
        for q in range(2):
            keep, give, take = finals(i, q)
            keep.wait()
            give.wait_send()
            take.wait_recv()


def body(
    in_weights, short_taps, long_taps, first_saved, second_saved, first_cotangent, last_cotangent
):
    anywhere = pl.BlockSpec(memory_space=pl.ANY)
    vmem = pl.BlockSpec(memory_space=pltpu.VMEM)
    dma = pltpu.SemaphoreType.DMA
    first, second = pl.pallas_call(
        kernel,
        out_shape=(jax.ShapeDtypeStruct((256, 1024), bf16),) * 2,
        in_specs=[anywhere, vmem, vmem, anywhere, anywhere, anywhere, anywhere, vmem, vmem, vmem],
        out_specs=(anywhere, anywhere),
        scratch_shapes=[
            pltpu.VMEM((8, 3, 256, 1024), bf16),
            pltpu.VMEM((2, 3, ROWS, 1024), bf16),
            pltpu.VMEM((2, REACH, 1024), bf16),
            pltpu.VMEM((REACH, 1024), f32),
            pltpu.VMEM((REACH, 1024), f32),
            pltpu.VMEM((REACH, 1024), f32),
            pltpu.VMEM((KEPT, 1024), f32),
            pltpu.VMEM((3, GROUP, 1024), bf16),
            pltpu.VMEM((8, GROUP, 256), bf16),
            pltpu.VMEM((2, 4, 2, GROUP, 256), bf16),
            pltpu.VMEM((2, 2, GROUP, 256), bf16),
            pltpu.VMEM((N, 1024), f32),
            pltpu.VMEM((REACH, CHUNK), bf16),
            pltpu.VMEM((REACH, CHUNK), bf16),
            pltpu.VMEM((3, KEPT, CHUNK), f32),
            dma((8,)), dma((8,)), dma((4,)), dma((4,)), dma((9,)),
            dma((2, 3, 2)), dma((2, 5)), dma((2, 8)), dma((2, 4, 2)),
            dma((2, 2)), dma((4,)), dma((2, 2)), dma((4,)), dma((2, 2)), dma((2, 2)),
        ],
        compiler_params=pltpu.CompilerParams(
            collective_id=0, has_side_effects=True, vmem_limit_bytes=60 * 1024 * 1024
        ),
    )(
        in_weights[0], short_taps[0], long_taps[0], first_saved[0], second_saved[0],
        first_cotangent[0], last_cotangent,
        FORWARD.astype(bf16), INVERSE.astype(bf16), FORWARD[:, :HALF],
    )
    return first[None], second[None]


def solution(mesh):
    in_specs = (
        P("section", None, "ctx", "tp"),
        P("section", None, None, "tp"),
        P("section", None, "tp"),
        P("section", None, "ctx", "tp"),
        P("section", None, "ctx", "tp"),
        P("section", "ctx", "tp"),
        P("ctx", "tp"),
    )
    out_specs = (P("section", "ctx", "tp"), P("section", "ctx", "tp"))
    return jax.shard_map(body, mesh=mesh, in_specs=in_specs, out_specs=out_specs, check_vma=False)
```

```python
import functools

import numpy as np
import jax
import jax.numpy as jnp
from jax import lax
from jax.experimental import pallas as pl
from jax.experimental.pallas import tpu as pltpu
from jax.sharding import PartitionSpec as P

MESH = pl.DeviceIdType.MESH
N = 256
HALF = 128
BEFORE = 144
AFTER = 160
GROUP = 512
ROWS = BEFORE + GROUP + AFTER
REACH = GROUP + AFTER
KEPT = GROUP + 16
CHUNK = 256
TILE = 32
FAR = 224
f32 = jnp.float32
bf16 = jnp.bfloat16


def shifted_dft():
    k = np.arange(HALF)[:, None] + 0.5
    n = np.arange(N)[None, :]
    angle = 2.0 * np.pi * k * n / N
    forward = np.concatenate([np.cos(angle), -np.sin(angle)], axis=0)
    return forward.astype(np.float32), (forward.T * (2.0 / N)).astype(np.float32)


FORWARD, INVERSE = shifted_dft()


def dot(a, b):
    return jnp.dot(a, b, preferred_element_type=f32)


def filtered(forward, inverse, signal, real, imag):
    spectrum = dot(forward, signal)
    a, b = spectrum[:HALF], spectrum[HALF:]
    mixed = jnp.concatenate([a * real - b * imag, a * imag + b * real], axis=0).astype(bf16)
    return dot(inverse, mixed)


def kernel(
    w_ref, short_ref, long_ref, u1_ref, u2_ref, g1_ref, gl_ref, fwd_ref, inv_ref, fwd32_ref,
    out1_ref, out2_ref,
    wb, ue, ge, p0, p1, p2, mx, di, pb, rb, tb, sb, resp, pr, dm, df,
    ring_s, ring_r, x_s, x_r, loc, halo_s, halo_r, pass_s, tp_s, tp_r, sum_s, sum_r, hop_r, main_s, main_r,
    edge_s, edge_r, fin_s, fin_r,
):
    s = lax.axis_index("section")
    c = lax.axis_index("ctx")
    k = lax.axis_index("tp")
    z, h = c // 2, c % 2
    up, down = (z + 1) % 8, (z + 7) % 8
    partner = 2 * z + 1 - h
    last = s == 3

    def remote(src, dst, send, recv, device):
        return pltpu.make_async_remote_copy(
            src_ref=src, dst_ref=dst, send_sem=send, recv_sem=recv,
            device_id=device, device_id_type=MESH,
        )

    barrier = pltpu.get_barrier_semaphore()

    def greet(device):
        pl.semaphore_signal(barrier, inc=1, device_id=device, device_id_type=MESH)

    greet({"ctx": partner})
    for zz in (up, down):
        for hh in range(2):
            greet({"ctx": 2 * zz + hh})
    for step in range(1, 4):
        greet({"tp": (k + step) % 4})

    @pl.when(s < 3)
    def _():
        for zz in (z, up):
            for hh in range(2):
                greet({"section": s + 1, "ctx": 2 * zz + hh})

    pl.semaphore_wait(barrier, 8 + 4 * ((s + 3) // 4))

    def ring(to_right, step, piece, rows=None):
        target = {"ctx": 2 * (up if to_right else down) + h}
        rows = rows or (128 * piece, 128)
        part = pl.ds(*rows)
        source = step if to_right else (8 - step) % 8
        dest = step + 1 if to_right else 7 - step
        src = w_ref.at[:, part] if step == 0 else wb.at[source, :, part]
        way = 0 if to_right else 1
        return remote(src, wb.at[dest, :, part], ring_s.at[way, step, piece], ring_r.at[way, step, piece], target)

    def ends(hh, piece):
        if hh == 0:
            return ring(True, 3, 0) if piece == 0 else ring(True, 3, 1, (128, FAR - 128))
        return ring(False, 3, 1) if piece == 1 else ring(False, 3, 0, (256 - FAR, FAR - 128))

    def short_end(hh):
        return ring(False, 3, 1, (FAR, 256 - FAR)) if hh == 0 else ring(True, 3, 0, (0, 256 - FAR))

    def by_column(act):
        for hh in range(2):
            pl.when(h == hh)(functools.partial(act, hh))

    def hand_on(step, turn):
        def act(hh):
            piece = turn if hh == 0 else 1 - turn
            for to_right in ((False, True) if hh == 1 else (True, False)):
                ring(to_right, step, piece).wait_recv()
                if step < 2:
                    ring(to_right, step + 1, piece).start()
                elif to_right == (hh == 0):
                    ends(hh, piece).start()
                elif turn == 1:
                    short_end(hh).start()

        by_column(act)

    def begin(hh):
        for turn in range(2):
            for to_right in (True, False):
                ring(to_right, 0, turn if hh == 0 else 1 - turn).start()

    by_column(begin)

    own_rows = pl.ds(pl.multiple_of(BEFORE + 256 * h, 16), 256)
    other_rows = pl.ds(pl.multiple_of(BEFORE + 256 * (1 - h), 16), 256)
    own_g = pl.ds(pl.multiple_of(256 * h, 256), 256)
    other_g = pl.ds(pl.multiple_of(256 * (1 - h), 256), 256)
    saved = (u1_ref, u2_ref)
    grads = (g1_ref, gl_ref)

    local_w = pltpu.make_async_copy(w_ref, wb.at[0], loc.at[0])
    local_u = [pltpu.make_async_copy(saved[i], ue.at[i, :, own_rows], loc.at[1 + i]) for i in range(2)]
    local_g = [pltpu.make_async_copy(grads[i], ge.at[i, own_g], loc.at[3 + i]) for i in range(2)]
    send_u = [
        remote(saved[i], ue.at[i, :, own_rows], x_s.at[i], x_r.at[i], {"ctx": partner}) for i in range(2)
    ]
    send_g = [
        remote(grads[i], ge.at[i, own_g], x_s.at[2 + i], x_r.at[2 + i], {"ctx": partner})
        for i in range(2)
    ]
    get_u = [
        remote(saved[i], ue.at[i, :, other_rows], x_s.at[i], x_r.at[i], {"ctx": partner}) for i in range(2)
    ]
    get_g = [
        remote(grads[i], ge.at[i, other_g], x_s.at[2 + i], x_r.at[2 + i], {"ctx": partner})
        for i in range(2)
    ]

    def before_parts(i):
        return [
            (saved[i].at[pl.ds(1, 2), pl.ds(256 - BEFORE, BEFORE)], ue.at[i, pl.ds(1, 2), pl.ds(0, BEFORE)], 0),
            (saved[i].at[0, pl.ds(240, 16)], ue.at[i, 0, pl.ds(BEFORE - 16, 16)], 1),
        ]

    def after_parts(i):
        return [
            (saved[i].at[0, pl.ds(0, AFTER)], ue.at[i, 0, pl.ds(BEFORE + GROUP, AFTER)], 2),
            (saved[i].at[pl.ds(1, 2), pl.ds(0, 32)], ue.at[i, pl.ds(1, 2), pl.ds(BEFORE + GROUP, 32)], 3),
        ]

    def grad_parts(i):
        return [(grads[i].at[pl.ds(0, AFTER)], ge.at[i, pl.ds(GROUP, AFTER)], 4)]

    def along(i, parts, to):
        return [remote(src, dst, halo_s.at[i, n], halo_r.at[i, n], {"ctx": to}) for src, dst, n in parts]

    def onward(i, parts):
        return [remote(dst, dst, pass_s.at[i, n], halo_r.at[i, n], {"ctx": partner}) for _, dst, n in parts]

    def start_halos(i, with_u, with_g):
        @pl.when(h == 1)
        def _():
            if with_u:
                for copy in along(i, before_parts(i), 2 * up + 1):
                    copy.start()

        @pl.when(h == 0)
        def _():
            for copy in along(i, after_parts(i) * with_u + grad_parts(i) * with_g, 2 * down):
                copy.start()

    def end_halos(i, with_u, with_g):
        @pl.when(h == 1)
        def _():
            if with_u:
                for copy in along(i, before_parts(i), 2 * up + 1) + onward(i, before_parts(i)):
                    copy.wait_send()

        @pl.when(h == 0)
        def _():
            parts = after_parts(i) * with_u + grad_parts(i) * with_g
            for copy in along(i, parts, 2 * down) + onward(i, parts):
                copy.wait_send()

    def pass_halos(i, with_u, with_g):
        @pl.when(h == 1)
        def _():
            if with_u:
                for copy in along(i, before_parts(i), 2 * up + 1):
                    copy.wait_recv()

                @pl.when(z == 0)
                def _():
                    ue[i, pl.ds(0, 3), pl.ds(BEFORE - 16, 16)] = jnp.zeros((3, 16, 1024), bf16)
                    ue[i, pl.ds(1, 2), pl.ds(0, BEFORE - 16)] = jnp.zeros((2, BEFORE - 16, 1024), bf16)

                for copy in onward(i, before_parts(i)):
                    copy.start()

        @pl.when(h == 0)
        def _():
            parts = after_parts(i) * with_u + grad_parts(i) * with_g
            for copy in along(i, parts, 2 * down):
                copy.wait_recv()

            if with_g:
                @pl.when(z == 7)
                def _():
                    ge[i, pl.ds(GROUP, AFTER)] = jnp.zeros((AFTER, 1024), bf16)

            for copy in onward(i, parts):
                copy.start()

    def receive_halos(i, with_u, with_g):
        @pl.when(h == 1)
        def _():
            for copy in onward(i, after_parts(i) * with_u + grad_parts(i) * with_g):
                copy.wait_recv()

        @pl.when(h == 0)
        def _():
            if with_u:
                for copy in onward(i, before_parts(i)):
                    copy.wait_recv()

    local_u[0].start()
    local_g[0].start()
    send_u[0].start()
    send_g[0].start()
    start_halos(0, True, True)
    local_w.start()
    local_u[1].start()

    @pl.when(last)
    def _():
        local_g[1].start()

    resp[...] = jnp.dot(
        fwd32_ref[...], long_ref[...], precision=lax.Precision.HIGHEST, preferred_element_type=f32
    )

    def columns(r):
        return pl.ds(pl.multiple_of(r * CHUNK, CHUNK), CHUNK)

    def features(i):
        def chunk(r, _):
            cols = columns(r)

            def short(m, x):
                total = x[16:] * short_ref[m, 0:1, cols]
                for tap in range(1, 7):
                    total += pltpu.roll(x, tap, 0)[16:] * short_ref[m, tap : tap + 1, cols]
                return total

            def tile(b, _):
                here = pl.ds(pl.multiple_of(b * TILE, TILE), TILE)
                wide = pl.ds(pl.multiple_of(b * TILE, TILE), TILE + 16)
                key = short(1, ue[i, 1, wide, cols].astype(f32))
                value = short(2, ue[i, 2, wide, cols].astype(f32))
                p1[here, cols] = key
                p2[here, cols] = value
                pr[here] = (key * value).astype(bf16)
                wide = pl.ds(pl.multiple_of(BEFORE - 16 + b * TILE, 16), TILE + 16)
                p0[here, cols] = short(0, ue[i, 0, wide, cols].astype(f32))
                return 0

            lax.fori_loop(0, REACH // TILE, tile, 0)
            real, imag = resp[:HALF, cols], resp[HALF:, cols]
            for b in range(4):
                mx[HALF * b : HALF * (b + 1), cols] = filtered(
                    fwd_ref[...], inv_ref[HALF:], pr[HALF * b : HALF * b + N], real, imag
                )
            mx[GROUP:KEPT, cols] = filtered(
                fwd_ref[:, :AFTER], inv_ref[HALF : HALF + 16], pr[GROUP:REACH], real, imag
            )
            return 0

        lax.fori_loop(0, 4, chunk, 0)

    def take_relay(r):
        cols = columns(r)

        @pl.when(s < 3)
        def _():
            remote(sb.at[0, 0], ge.at[1, pl.ds(0, GROUP), cols], main_s.at[0, 0], main_r.at[r],
                   {"ctx": partner}).wait_recv()
            remote(sb.at[0, 0, pl.ds(0, AFTER)], ge.at[1, pl.ds(GROUP, AFTER), cols], edge_s.at[0, 0],
                   edge_r.at[r], {"ctx": partner}).wait_recv()

            @pl.when(z == 7)
            def _():
                ge[1, pl.ds(GROUP, AFTER), cols] = jnp.zeros((AFTER, CHUNK), bf16)

    def gradients(i):
        def chunk(r, _):
            cols = columns(r)
            if i == 1:
                take_relay(r)

            def scale(b, _):
                here = pl.ds(pl.multiple_of(b * TILE, TILE), TILE)
                dm[here] = (ge[i, here, cols].astype(f32) * p0[here, cols]).astype(bf16)
                return 0

            lax.fori_loop(0, REACH // TILE, scale, 0)
            real, imag = resp[:HALF, cols], -resp[HALF:, cols]
            for b in range(5):
                rows = HALF if b < 4 else 16
                span = N if b < 4 else AFTER
                begin = HALF * b
                dproduct = filtered(
                    fwd_ref[:, :span], inv_ref[:rows], dm[begin : begin + span], real, imag
                )
                there = slice(begin, begin + rows)
                shifted = slice(begin + HALF, begin + HALF + rows)
                df[0, there] = ge[i, there, cols].astype(f32) * mx[there, cols]
                df[1, there] = dproduct * p2[shifted, cols]
                df[2, there] = dproduct * p1[shifted, cols]

            def tile(n, _):
                b, side = n // 2, n % 2
                here = pl.ds(pl.multiple_of(b * HALF, HALF), HALF)
                wide = pl.ds(pl.multiple_of(b * HALF, HALF), HALF + 8)
                part = pl.ds(pl.multiple_of(side * 128, 128), 128)
                there = pl.ds(pl.multiple_of(r * CHUNK + side * 128, 128), 128)
                for m in range(3):
                    x = df[m, wide, part]
                    total = x[:HALF] * short_ref[m, 0:1, there]
                    for tap in range(1, 7):
                        total += pltpu.roll(x, HALF + 8 - tap, 0)[:HALF] * short_ref[m, tap : tap + 1, there]
                    di[m, here, there] = total.astype(bf16)
                return 0

            lax.fori_loop(0, 8, tile, 0)
            return 0

        lax.fori_loop(0, 4, chunk, 0)

    def place(j):
        zt = (z + 8 - j) % 8
        return zt // 2, zt % 2

    def half_copy(j, half):
        kt, q = place(j)
        cols = pl.ds(128 * half if isinstance(half, int) else pl.multiple_of(128 * half, 128), 128)
        return remote(pb.at[j, :, cols], rb.at[0, k, q, :, cols], tp_s.at[j, half], tp_r.at[k, q, half], {"tp": kt})

    def end_first(j):
        kt, _ = place(j)

        @pl.when(kt != k)
        def _():
            for half in range(2):
                half_copy(j, half).wait_send()

    def end_second(j):
        kt, q = place(j)

        @pl.when(kt != k)
        def _():
            remote(pb.at[j], rb.at[1, k, q], sum_s.at[j], sum_r.at[k, q], {"tp": kt}).wait_send()

    def product(j):
        total = None
        for m in range(3):
            term = lax.dot_general(di[m], wb[j, m], (((1,), (1,)), ((), ())), preferred_element_type=f32)
            total = term if total is None else total + term
        return total.astype(bf16)

    def multiply_first(lo, hi):
        def unit(n, _):
            odd = n % 2
            j = odd * ((n + 1) // 2) + (1 - odd) * ((8 - n // 2) % 8)
            pb[j] = product(j)
            kt, _q = place(j)

            @pl.when(kt != k)
            def _():
                for half in range(2):
                    half_copy(j, half).start()

            return 0

        lax.fori_loop(lo, hi, unit, 0)

    def multiply_half(turn):
        half = turn * (1 - h) + (1 - turn) * h
        rows = pl.ds(pl.multiple_of(128 * half, 128), 128)
        total = None
        for m in range(3):
            term = lax.dot_general(
                di[m], wb[4, m, rows], (((1,), (1,)), ((), ())), preferred_element_type=f32
            )
            total = term if total is None else total + term
        pb[4, :, rows] = total.astype(bf16)
        kt, _ = place(4)

        @pl.when(kt != k)
        def _():
            half_copy(4, half).start()

    def multiply_second():
        def unit(n, _):
            odd, pair = n % 2, n // 2
            away = jnp.where(pair == 0, 2, jnp.where(pair == 2, 0, 1 + 2 * odd))
            q = jnp.where(pair == 1, 1 - odd, odd)
            target = (k + away) % 4
            j = (z + 8 - 2 * target - q) % 8
            end_first(j)
            pb[j] = product(j)

            @pl.when(n < 2)
            def _():
                remote(pb.at[j], tb.at[q], sum_s.at[j], hop_r.at[q], {"tp": (k + 1 + 2 * q) % 4}).start()

            @pl.when(n >= 6)
            def _():
                remote(pb.at[j], tb.at[q], sum_s.at[j], hop_r.at[q], {"tp": target}).wait_recv()
                pb[j] = (pb[j].astype(f32) + tb[q].astype(f32)).astype(bf16)

            @pl.when((pair == 1) | (pair == 3))
            def _():
                remote(pb.at[j], rb.at[1, k, q], sum_s.at[j], sum_r.at[k, q], {"tp": target}).start()

            return 0

        lax.fori_loop(0, 8, unit, 0)

    def combine(i, q):
        cols = columns(h + 2 * q)
        steps = (1, 2, 3) if i == 0 else (1, 3)
        for step in steps:
            src = (k + step) % 4
            if i == 1:
                remote(pb.at[0], rb.at[1, src, q], sum_s.at[0], sum_r.at[src, q], {"tp": src}).wait_recv()
                continue
            for half in range(2):
                part = pl.ds(128 * half, 128)
                remote(pb.at[0, :, part], rb.at[0, src, q, :, part], tp_s.at[0, half],
                       tp_r.at[src, q, half], {"tp": src}).wait_recv()
        mine = (z + 8 - 2 * k - q) % 8

        def tile(b, _):
            here = pl.ds(pl.multiple_of(b * 64, 64), 64)
            total = ge[i, here, cols].astype(f32) + pb[mine, here].astype(f32)
            for step in steps:
                total += rb[i, (k + step) % 4, q, here].astype(f32)
            sb[i, q, here] = total.astype(bf16)
            return 0

        lax.fori_loop(0, GROUP // 64, tile, 0)

    outs = (out1_ref, out2_ref)

    def finals(i, q):
        mine, theirs = columns(h + 2 * q), columns(1 - h + 2 * q)
        keep = pltpu.make_async_copy(sb.at[i, q, own_g], outs[i].at[:, mine], loc.at[5 + 2 * i + q])
        give = remote(sb.at[i, q, other_g], outs[i].at[:, mine], fin_s.at[i, q], fin_r.at[i, q], {"ctx": partner})
        take = remote(sb.at[i, q, other_g], outs[i].at[:, theirs], fin_s.at[i, q], fin_r.at[i, q], {"ctx": partner})
        return keep, give, take

    def relay(q, hh):
        r = h + 2 * q
        to = {"section": lax.rem(s + 3, 4), "ctx": 2 * z + hh}
        edge_to = {"section": lax.rem(s + 3, 4), "ctx": 2 * down + hh}
        return (
            remote(sb.at[0, q], ge.at[1, pl.ds(0, GROUP), columns(r)], main_s.at[q, hh], main_r.at[r], to),
            remote(sb.at[0, q, pl.ds(0, AFTER)], ge.at[1, pl.ds(GROUP, AFTER), columns(r)],
                   edge_s.at[q, hh], edge_r.at[r], edge_to),
        )

    hand_on(0, 0)
    hand_on(0, 1)
    pass_halos(0, True, True)
    local_u[0].wait()
    local_g[0].wait()
    get_u[0].wait_recv()
    get_g[0].wait_recv()
    send_u[1].start()
    start_halos(1, True, False)

    @pl.when(last)
    def _():
        send_g[1].start()
        start_halos(1, False, True)

    receive_halos(0, True, True)
    hand_on(1, 0)
    features(0)
    hand_on(1, 1)
    gradients(0)
    local_w.wait()
    multiply_first(0, 5)
    pass_halos(1, True, False)

    @pl.when(last)
    def _():
        pass_halos(1, False, True)

    hand_on(2, 0)
    local_u[1].wait()
    get_u[1].wait_recv()
    receive_halos(1, True, False)
    features(1)
    hand_on(2, 1)

    @pl.when(last)
    def _():
        local_g[1].wait()
        get_g[1].wait_recv()
        receive_halos(1, False, True)

    multiply_first(5, 7)
    by_column(lambda hh: ends(hh, hh).wait_recv())
    multiply_half(0)

    def arrive(hh):
        ends(hh, 1 - hh).wait_recv()
        short_end(hh).wait_recv()

    by_column(arrive)
    multiply_half(1)
    for q in range(2):
        combine(0, q)

        @pl.when(s > 0)
        def _():
            for copy in relay(q, 0) + relay(q, 1):
                copy.start()

    for q in range(2):
        keep, give, _ = finals(0, q)
        keep.start()
        give.start()

    gradients(1)
    multiply_second()
    for q in range(2):
        combine(1, q)
        keep, give, _ = finals(1, q)
        give.start()
        keep.start()

    def sent(hh):
        for to_right in (True, False):
            for step in range(3):
                for piece in range(2):
                    ring(to_right, step, piece).wait_send()
        for copy in (ends(hh, 0), ends(hh, 1), short_end(hh)):
            copy.wait_send()

    by_column(sent)
    for i in range(2):
        send_u[i].wait_send()
        end_halos(i, True, i == 0)
    send_g[0].wait_send()

    @pl.when(last)
    def _():
        send_g[1].wait_send()
        end_halos(1, False, True)

    @pl.when(s > 0)
    def _():
        for q in range(2):
            for copy in relay(q, 0) + relay(q, 1):
                copy.wait_send()

    def finish(j, _):
        end_second(j)
        return 0

    lax.fori_loop(0, 8, finish, 0)
    for i in range(2):
        for q in range(2):
            keep, give, take = finals(i, q)
            keep.wait()
            give.wait_send()
            take.wait_recv()


def body(
    in_weights, short_taps, long_taps, first_saved, second_saved, first_cotangent, last_cotangent
):
    anywhere = pl.BlockSpec(memory_space=pl.ANY)
    vmem = pl.BlockSpec(memory_space=pltpu.VMEM)
    dma = pltpu.SemaphoreType.DMA
    first, second = pl.pallas_call(
        kernel,
        out_shape=(jax.ShapeDtypeStruct((256, 1024), bf16),) * 2,
        in_specs=[anywhere, vmem, vmem, anywhere, anywhere, anywhere, anywhere, vmem, vmem, vmem],
        out_specs=(anywhere, anywhere),
        scratch_shapes=[
            pltpu.VMEM((8, 3, 256, 1024), bf16),
            pltpu.VMEM((2, 3, ROWS, 1024), bf16),
            pltpu.VMEM((2, REACH, 1024), bf16),
            pltpu.VMEM((REACH, 1024), f32),
            pltpu.VMEM((REACH, 1024), f32),
            pltpu.VMEM((REACH, 1024), f32),
            pltpu.VMEM((KEPT, 1024), f32),
            pltpu.VMEM((3, GROUP, 1024), bf16),
            pltpu.VMEM((8, GROUP, 256), bf16),
            pltpu.VMEM((2, 4, 2, GROUP, 256), bf16),
            pltpu.VMEM((2, GROUP, 256), bf16),
            pltpu.VMEM((2, 2, GROUP, 256), bf16),
            pltpu.VMEM((N, 1024), f32),
            pltpu.VMEM((REACH, CHUNK), bf16),
            pltpu.VMEM((REACH, CHUNK), bf16),
            pltpu.VMEM((3, KEPT, CHUNK), f32),
            dma((2, 4, 2)), dma((2, 4, 2)), dma((4,)), dma((4,)), dma((9,)),
            dma((2, 5)), dma((2, 5)), dma((2, 5)), dma((8, 2)), dma((4, 2, 2)), dma((8,)), dma((4, 2)), dma((2,)),
            dma((2, 2)), dma((4,)), dma((2, 2)), dma((4,)), dma((2, 2)), dma((2, 2)),
        ],
        compiler_params=pltpu.CompilerParams(
            collective_id=0, has_side_effects=True, vmem_limit_bytes=60 * 1024 * 1024
        ),
    )(
        in_weights[0], short_taps[0], long_taps[0], first_saved[0], second_saved[0],
        first_cotangent[0], last_cotangent,
        FORWARD.astype(bf16), INVERSE.astype(bf16), FORWARD[:, :HALF],
    )
    return first[None], second[None]


def solution(mesh):
    in_specs = (
        P("section", None, "ctx", "tp"),
        P("section", None, None, "tp"),
        P("section", None, "tp"),
        P("section", None, "ctx", "tp"),
        P("section", None, "ctx", "tp"),
        P("section", "ctx", "tp"),
        P("ctx", "tp"),
    )
    out_specs = (P("section", "ctx", "tp"), P("section", "ctx", "tp"))
    return jax.shard_map(body, mesh=mesh, in_specs=in_specs, out_specs=out_specs, check_vma=False)
```

```python
import functools

import numpy as np
import jax
import jax.numpy as jnp
from jax import lax
from jax.experimental import pallas as pl
from jax.experimental.pallas import tpu as pltpu
from jax.sharding import PartitionSpec as P

MESH = pl.DeviceIdType.MESH
N = 256
HALF = 128
BEFORE = 144
AFTER = 160
GROUP = 512
ROWS = BEFORE + GROUP + AFTER
REACH = GROUP + AFTER
KEPT = GROUP + 16
CHUNK = 256
TILE = 32
FAR = 224
f32 = jnp.float32
bf16 = jnp.bfloat16


def shifted_dft():
    k = np.arange(HALF)[:, None] + 0.5
    n = np.arange(N)[None, :]
    angle = 2.0 * np.pi * k * n / N
    forward = np.concatenate([np.cos(angle), -np.sin(angle)], axis=0)
    return forward.astype(np.float32), (forward.T * (2.0 / N)).astype(np.float32)


FORWARD, INVERSE = shifted_dft()


def dot(a, b):
    return jnp.dot(a, b, preferred_element_type=f32)


def filtered(forward, inverse, signal, real, imag):
    spectrum = dot(forward, signal)
    a, b = spectrum[:HALF], spectrum[HALF:]
    mixed = jnp.concatenate([a * real - b * imag, a * imag + b * real], axis=0).astype(bf16)
    return dot(inverse, mixed)


def kernel(
    w_ref, short_ref, long_ref, u1_ref, u2_ref, g1_ref, gl_ref, fwd_ref, inv_ref, fwd32_ref,
    out1_ref, out2_ref,
    wb, ue, ge, p0, p1, p2, mx, di, pb, rb, tb, sb, resp, pr, dm, df,
    ring_s, ring_r, x_s, x_r, loc, halo_s, halo_r, pass_s, tp_s, tp_r, sum_s, sum_r, hop_r, main_s, main_r,
    edge_s, edge_r, fin_s, fin_r,
):
    s = lax.axis_index("section")
    c = lax.axis_index("ctx")
    k = lax.axis_index("tp")
    z, h = c // 2, c % 2
    up, down = (z + 1) % 8, (z + 7) % 8
    partner = 2 * z + 1 - h
    last = s == 3

    def remote(src, dst, send, recv, device):
        return pltpu.make_async_remote_copy(
            src_ref=src, dst_ref=dst, send_sem=send, recv_sem=recv,
            device_id=device, device_id_type=MESH,
        )

    barrier = pltpu.get_barrier_semaphore()

    def greet(device):
        pl.semaphore_signal(barrier, inc=1, device_id=device, device_id_type=MESH)

    greet({"ctx": partner})
    for zz in (up, down):
        for hh in range(2):
            greet({"ctx": 2 * zz + hh})
    for step in range(1, 4):
        greet({"tp": (k + step) % 4})

    @pl.when(s < 3)
    def _():
        for zz in (z, up):
            for hh in range(2):
                greet({"section": s + 1, "ctx": 2 * zz + hh})

    pl.semaphore_wait(barrier, 8 + 4 * ((s + 3) // 4))

    def ring(to_right, step, piece, rows=None):
        target = {"ctx": 2 * (up if to_right else down) + h}
        rows = rows or (128 * piece, 128)
        part = pl.ds(*rows)
        source = step if to_right else (8 - step) % 8
        dest = step + 1 if to_right else 7 - step
        src = w_ref.at[:, part] if step == 0 else wb.at[source, :, part]
        way = 0 if to_right else 1
        return remote(src, wb.at[dest, :, part], ring_s.at[way, step, piece], ring_r.at[way, step, piece], target)

    def ends(hh, piece):
        if hh == 0:
            return ring(True, 3, 0) if piece == 0 else ring(True, 3, 1, (128, FAR - 128))
        return ring(False, 3, 1) if piece == 1 else ring(False, 3, 0, (256 - FAR, FAR - 128))

    def short_end(hh):
        return ring(False, 3, 1, (FAR, 256 - FAR)) if hh == 0 else ring(True, 3, 0, (0, 256 - FAR))

    def by_column(act):
        for hh in range(2):
            pl.when(h == hh)(functools.partial(act, hh))

    def hand_on(step, turn):
        def act(hh):
            piece = turn if hh == 0 else 1 - turn
            for to_right in ((False, True) if hh == 1 else (True, False)):
                ring(to_right, step, piece).wait_recv()
                if step < 2:
                    ring(to_right, step + 1, piece).start()
                elif to_right == (hh == 0):
                    ends(hh, piece).start()
                elif turn == 1:
                    short_end(hh).start()

        by_column(act)

    def begin(hh):
        for turn in range(2):
            for to_right in (True, False):
                ring(to_right, 0, turn if hh == 0 else 1 - turn).start()

    by_column(begin)

    own_rows = pl.ds(pl.multiple_of(BEFORE + 256 * h, 16), 256)
    other_rows = pl.ds(pl.multiple_of(BEFORE + 256 * (1 - h), 16), 256)
    own_g = pl.ds(pl.multiple_of(256 * h, 256), 256)
    other_g = pl.ds(pl.multiple_of(256 * (1 - h), 256), 256)
    saved = (u1_ref, u2_ref)
    grads = (g1_ref, gl_ref)

    local_w = pltpu.make_async_copy(w_ref, wb.at[0], loc.at[0])
    local_u = [pltpu.make_async_copy(saved[i], ue.at[i, :, own_rows], loc.at[1 + i]) for i in range(2)]
    local_g = [pltpu.make_async_copy(grads[i], ge.at[i, own_g], loc.at[3 + i]) for i in range(2)]
    send_u = [
        remote(saved[i], ue.at[i, :, own_rows], x_s.at[i], x_r.at[i], {"ctx": partner}) for i in range(2)
    ]
    send_g = [
        remote(grads[i], ge.at[i, own_g], x_s.at[2 + i], x_r.at[2 + i], {"ctx": partner})
        for i in range(2)
    ]
    get_u = [
        remote(saved[i], ue.at[i, :, other_rows], x_s.at[i], x_r.at[i], {"ctx": partner}) for i in range(2)
    ]
    get_g = [
        remote(grads[i], ge.at[i, other_g], x_s.at[2 + i], x_r.at[2 + i], {"ctx": partner})
        for i in range(2)
    ]

    def before_parts(i):
        return [
            (saved[i].at[pl.ds(1, 2), pl.ds(256 - BEFORE, BEFORE)], ue.at[i, pl.ds(1, 2), pl.ds(0, BEFORE)], 0),
            (saved[i].at[0, pl.ds(240, 16)], ue.at[i, 0, pl.ds(BEFORE - 16, 16)], 1),
        ]

    def after_parts(i):
        return [
            (saved[i].at[0, pl.ds(0, AFTER)], ue.at[i, 0, pl.ds(BEFORE + GROUP, AFTER)], 2),
            (saved[i].at[pl.ds(1, 2), pl.ds(0, 32)], ue.at[i, pl.ds(1, 2), pl.ds(BEFORE + GROUP, 32)], 3),
        ]

    def grad_parts(i):
        return [(grads[i].at[pl.ds(0, AFTER)], ge.at[i, pl.ds(GROUP, AFTER)], 4)]

    def along(i, parts, to):
        return [remote(src, dst, halo_s.at[i, n], halo_r.at[i, n], {"ctx": to}) for src, dst, n in parts]

    def onward(i, parts):
        return [remote(dst, dst, pass_s.at[i, n], halo_r.at[i, n], {"ctx": partner}) for _, dst, n in parts]

    def start_halos(i, with_u, with_g):
        @pl.when(h == 1)
        def _():
            if with_u:
                for copy in along(i, before_parts(i), 2 * up + 1):
                    copy.start()

        @pl.when(h == 0)
        def _():
            for copy in along(i, after_parts(i) * with_u + grad_parts(i) * with_g, 2 * down):
                copy.start()

    def end_halos(i, with_u, with_g):
        @pl.when(h == 1)
        def _():
            if with_u:
                for copy in along(i, before_parts(i), 2 * up + 1) + onward(i, before_parts(i)):
                    copy.wait_send()

        @pl.when(h == 0)
        def _():
            parts = after_parts(i) * with_u + grad_parts(i) * with_g
            for copy in along(i, parts, 2 * down) + onward(i, parts):
                copy.wait_send()

    def pass_halos(i, with_u, with_g):
        @pl.when(h == 1)
        def _():
            if with_u:
                for copy in along(i, before_parts(i), 2 * up + 1):
                    copy.wait_recv()

                @pl.when(z == 0)
                def _():
                    ue[i, pl.ds(0, 3), pl.ds(BEFORE - 16, 16)] = jnp.zeros((3, 16, 1024), bf16)
                    ue[i, pl.ds(1, 2), pl.ds(0, BEFORE - 16)] = jnp.zeros((2, BEFORE - 16, 1024), bf16)

                for copy in onward(i, before_parts(i)):
                    copy.start()

        @pl.when(h == 0)
        def _():
            parts = after_parts(i) * with_u + grad_parts(i) * with_g
            for copy in along(i, parts, 2 * down):
                copy.wait_recv()

            if with_g:
                @pl.when(z == 7)
                def _():
                    ge[i, pl.ds(GROUP, AFTER)] = jnp.zeros((AFTER, 1024), bf16)

            for copy in onward(i, parts):
                copy.start()

    def receive_halos(i, with_u, with_g):
        @pl.when(h == 1)
        def _():
            for copy in onward(i, after_parts(i) * with_u + grad_parts(i) * with_g):
                copy.wait_recv()

        @pl.when(h == 0)
        def _():
            if with_u:
                for copy in onward(i, before_parts(i)):
                    copy.wait_recv()

    local_u[0].start()
    local_g[0].start()
    send_u[0].start()
    send_g[0].start()
    start_halos(0, True, True)
    local_w.start()
    local_u[1].start()

    @pl.when(last)
    def _():
        local_g[1].start()

    resp[...] = jnp.dot(
        fwd32_ref[...], long_ref[...], precision=lax.Precision.HIGHEST, preferred_element_type=f32
    )

    def columns(r):
        return pl.ds(pl.multiple_of(r * CHUNK, CHUNK), CHUNK)

    def features(i):
        def chunk(r, _):
            cols = columns(r)

            def short(m, x):
                total = x[16:] * short_ref[m, 0:1, cols]
                for tap in range(1, 7):
                    total += pltpu.roll(x, tap, 0)[16:] * short_ref[m, tap : tap + 1, cols]
                return total

            def tile(b, _):
                here = pl.ds(pl.multiple_of(b * TILE, TILE), TILE)
                wide = pl.ds(pl.multiple_of(b * TILE, TILE), TILE + 16)
                key = short(1, ue[i, 1, wide, cols].astype(f32))
                value = short(2, ue[i, 2, wide, cols].astype(f32))
                p1[here, cols] = key
                p2[here, cols] = value
                pr[here] = (key * value).astype(bf16)
                wide = pl.ds(pl.multiple_of(BEFORE - 16 + b * TILE, 16), TILE + 16)
                p0[here, cols] = short(0, ue[i, 0, wide, cols].astype(f32))
                return 0

            lax.fori_loop(0, REACH // TILE, tile, 0)
            real, imag = resp[:HALF, cols], resp[HALF:, cols]
            for b in range(4):
                mx[HALF * b : HALF * (b + 1), cols] = filtered(
                    fwd_ref[...], inv_ref[HALF:], pr[HALF * b : HALF * b + N], real, imag
                )
            mx[GROUP:KEPT, cols] = filtered(
                fwd_ref[:, :AFTER], inv_ref[HALF : HALF + 16], pr[GROUP:REACH], real, imag
            )
            return 0

        lax.fori_loop(0, 4, chunk, 0)

    def take_relay(r):
        cols = columns(r)

        @pl.when(s < 3)
        def _():
            remote(sb.at[0, 0], ge.at[1, pl.ds(0, GROUP), cols], main_s.at[0, 0], main_r.at[r],
                   {"ctx": partner}).wait_recv()
            remote(sb.at[0, 0, pl.ds(0, AFTER)], ge.at[1, pl.ds(GROUP, AFTER), cols], edge_s.at[0, 0],
                   edge_r.at[r], {"ctx": partner}).wait_recv()

            @pl.when(z == 7)
            def _():
                ge[1, pl.ds(GROUP, AFTER), cols] = jnp.zeros((AFTER, CHUNK), bf16)

    def gradients(i):
        def chunk(r, _):
            cols = columns(r)
            if i == 1:
                take_relay(r)

            def scale(b, _):
                here = pl.ds(pl.multiple_of(b * TILE, TILE), TILE)
                dm[here] = (ge[i, here, cols].astype(f32) * p0[here, cols]).astype(bf16)
                return 0

            lax.fori_loop(0, REACH // TILE, scale, 0)
            real, imag = resp[:HALF, cols], -resp[HALF:, cols]
            for b in range(5):
                rows = HALF if b < 4 else 16
                span = N if b < 4 else AFTER
                begin = HALF * b
                dproduct = filtered(
                    fwd_ref[:, :span], inv_ref[:rows], dm[begin : begin + span], real, imag
                )
                there = slice(begin, begin + rows)
                shifted = slice(begin + HALF, begin + HALF + rows)
                df[0, there] = ge[i, there, cols].astype(f32) * mx[there, cols]
                df[1, there] = dproduct * p2[shifted, cols]
                df[2, there] = dproduct * p1[shifted, cols]

            def tile(n, _):
                b, side = n // 2, n % 2
                here = pl.ds(pl.multiple_of(b * HALF, HALF), HALF)
                wide = pl.ds(pl.multiple_of(b * HALF, HALF), HALF + 8)
                part = pl.ds(pl.multiple_of(side * 128, 128), 128)
                there = pl.ds(pl.multiple_of(r * CHUNK + side * 128, 128), 128)
                for m in range(3):
                    x = df[m, wide, part]
                    total = x[:HALF] * short_ref[m, 0:1, there]
                    for tap in range(1, 7):
                        total += pltpu.roll(x, HALF + 8 - tap, 0)[:HALF] * short_ref[m, tap : tap + 1, there]
                    di[m, here, there] = total.astype(bf16)
                return 0

            lax.fori_loop(0, 8, tile, 0)
            return 0

        lax.fori_loop(0, 4, chunk, 0)

    def place(j):
        zt = (z + 8 - j) % 8
        return zt // 2, zt % 2

    def half_copy(j, half):
        kt, q = place(j)
        cols = pl.ds(128 * half if isinstance(half, int) else pl.multiple_of(128 * half, 128), 128)
        return remote(pb.at[j, :, cols], rb.at[0, k, q, :, cols], tp_s.at[j, half], tp_r.at[k, q, half], {"tp": kt})

    def end_first(j):
        kt, _ = place(j)

        @pl.when(kt != k)
        def _():
            for half in range(2):
                half_copy(j, half).wait_send()

    def end_second(j):
        kt, q = place(j)

        @pl.when(kt != k)
        def _():
            remote(pb.at[j], rb.at[1, k, q], sum_s.at[j], sum_r.at[k, q], {"tp": kt}).wait_send()

    def product(j):
        total = None
        for m in range(3):
            term = lax.dot_general(di[m], wb[j, m], (((1,), (1,)), ((), ())), preferred_element_type=f32)
            total = term if total is None else total + term
        return total.astype(bf16)

    def multiply_first(lo, hi):
        def unit(n, _):
            odd = n % 2
            j = odd * ((n + 1) // 2) + (1 - odd) * ((8 - n // 2) % 8)
            pb[j] = product(j)
            kt, _q = place(j)

            @pl.when(kt != k)
            def _():
                for half in range(2):
                    half_copy(j, half).start()

            return 0

        lax.fori_loop(lo, hi, unit, 0)

    def multiply_half(turn):
        half = turn * (1 - h) + (1 - turn) * h
        rows = pl.ds(pl.multiple_of(128 * half, 128), 128)
        total = None
        for m in range(3):
            term = lax.dot_general(
                di[m], wb[4, m, rows], (((1,), (1,)), ((), ())), preferred_element_type=f32
            )
            total = term if total is None else total + term
        pb[4, :, rows] = total.astype(bf16)
        kt, _ = place(4)

        @pl.when(kt != k)
        def _():
            half_copy(4, half).start()

    def multiply_second():
        def unit(n, _):
            odd, pair = n % 2, n // 2
            away = jnp.where(pair == 0, 2, jnp.where(pair == 2, 0, 1 + 2 * odd))
            q = jnp.where(pair == 1, 1 - odd, odd)
            target = (k + away) % 4
            j = (z + 8 - 2 * target - q) % 8
            end_first(j)
            pb[j] = product(j)

            @pl.when(n < 2)
            def _():
                remote(pb.at[j], tb.at[q], sum_s.at[j], hop_r.at[q], {"tp": (k + 1 + 2 * q) % 4}).start()

            @pl.when(n >= 6)
            def _():
                remote(pb.at[j], tb.at[q], sum_s.at[j], hop_r.at[q], {"tp": target}).wait_recv()
                pb[j] = (pb[j].astype(f32) + tb[q].astype(f32)).astype(bf16)

            @pl.when((pair == 1) | (pair == 3))
            def _():
                remote(pb.at[j], rb.at[1, k, q], sum_s.at[j], sum_r.at[k, q], {"tp": target}).start()

            return 0

        lax.fori_loop(0, 8, unit, 0)

    def combine(i, q):
        cols = columns(h + 2 * q)
        steps = (1, 2, 3) if i == 0 else (1, 3)
        for step in steps:
            src = (k + step) % 4
            if i == 1:
                remote(pb.at[0], rb.at[1, src, q], sum_s.at[0], sum_r.at[src, q], {"tp": src}).wait_recv()
                continue
            for half in range(2):
                part = pl.ds(128 * half, 128)
                remote(pb.at[0, :, part], rb.at[0, src, q, :, part], tp_s.at[0, half],
                       tp_r.at[src, q, half], {"tp": src}).wait_recv()
        mine = (z + 8 - 2 * k - q) % 8

        def tile(b, _):
            here = pl.ds(pl.multiple_of(b * 64, 64), 64)
            total = ge[i, here, cols].astype(f32) + pb[mine, here].astype(f32)
            for step in steps:
                total += rb[i, (k + step) % 4, q, here].astype(f32)
            sb[i, q, here] = total.astype(bf16)
            return 0

        lax.fori_loop(0, GROUP // 64, tile, 0)

    outs = (out1_ref, out2_ref)

    def finals(i, q):
        mine, theirs = columns(h + 2 * q), columns(1 - h + 2 * q)
        keep = pltpu.make_async_copy(sb.at[i, q, own_g], outs[i].at[:, mine], loc.at[5 + 2 * i + q])
        give = remote(sb.at[i, q, other_g], outs[i].at[:, mine], fin_s.at[i, q], fin_r.at[i, q], {"ctx": partner})
        take = remote(sb.at[i, q, other_g], outs[i].at[:, theirs], fin_s.at[i, q], fin_r.at[i, q], {"ctx": partner})
        return keep, give, take

    def relay(q, hh):
        r = h + 2 * q
        to = {"section": lax.rem(s + 3, 4), "ctx": 2 * z + hh}
        edge_to = {"section": lax.rem(s + 3, 4), "ctx": 2 * down + hh}
        return (
            remote(sb.at[0, q], ge.at[1, pl.ds(0, GROUP), columns(r)], main_s.at[q, hh], main_r.at[r], to),
            remote(sb.at[0, q, pl.ds(0, AFTER)], ge.at[1, pl.ds(GROUP, AFTER), columns(r)],
                   edge_s.at[q, hh], edge_r.at[r], edge_to),
        )

    hand_on(0, 0)
    hand_on(0, 1)
    pass_halos(0, True, True)
    local_u[0].wait()
    local_g[0].wait()
    get_u[0].wait_recv()
    get_g[0].wait_recv()
    send_u[1].start()
    start_halos(1, True, False)

    @pl.when(last)
    def _():
        send_g[1].start()
        start_halos(1, False, True)

    receive_halos(0, True, True)
    hand_on(1, 0)
    features(0)
    hand_on(1, 1)
    gradients(0)
    local_w.wait()
    multiply_first(0, 5)
    pass_halos(1, True, False)

    @pl.when(last)
    def _():
        pass_halos(1, False, True)

    hand_on(2, 0)
    local_u[1].wait()
    get_u[1].wait_recv()
    receive_halos(1, True, False)
    features(1)
    hand_on(2, 1)

    @pl.when(last)
    def _():
        local_g[1].wait()
        get_g[1].wait_recv()
        receive_halos(1, False, True)

    multiply_first(5, 7)
    by_column(lambda hh: ends(hh, hh).wait_recv())
    multiply_half(0)

    def arrive(hh):
        ends(hh, 1 - hh).wait_recv()
        short_end(hh).wait_recv()

    by_column(arrive)
    multiply_half(1)
    for q in range(2):
        combine(0, q)

        @pl.when(s > 0)
        def _():
            for copy in relay(q, 0) + relay(q, 1):
                copy.start()

    gradients(1)
    for q in range(2):
        keep, give, _ = finals(0, q)
        keep.start()
        give.start()
    multiply_second()
    for q in range(2):
        combine(1, q)
        keep, give, _ = finals(1, q)
        give.start()
        keep.start()

    def sent(hh):
        for to_right in (True, False):
            for step in range(3):
                for piece in range(2):
                    ring(to_right, step, piece).wait_send()
        for copy in (ends(hh, 0), ends(hh, 1), short_end(hh)):
            copy.wait_send()

    by_column(sent)
    for i in range(2):
        send_u[i].wait_send()
        end_halos(i, True, i == 0)
    send_g[0].wait_send()

    @pl.when(last)
    def _():
        send_g[1].wait_send()
        end_halos(1, False, True)

    @pl.when(s > 0)
    def _():
        for q in range(2):
            for copy in relay(q, 0) + relay(q, 1):
                copy.wait_send()

    def finish(j, _):
        end_second(j)
        return 0

    lax.fori_loop(0, 8, finish, 0)
    for i in range(2):
        for q in range(2):
            keep, give, take = finals(i, q)
            keep.wait()
            give.wait_send()
            take.wait_recv()


def body(
    in_weights, short_taps, long_taps, first_saved, second_saved, first_cotangent, last_cotangent
):
    anywhere = pl.BlockSpec(memory_space=pl.ANY)
    vmem = pl.BlockSpec(memory_space=pltpu.VMEM)
    dma = pltpu.SemaphoreType.DMA
    first, second = pl.pallas_call(
        kernel,
        out_shape=(jax.ShapeDtypeStruct((256, 1024), bf16),) * 2,
        in_specs=[anywhere, vmem, vmem, anywhere, anywhere, anywhere, anywhere, vmem, vmem, vmem],
        out_specs=(anywhere, anywhere),
        scratch_shapes=[
            pltpu.VMEM((8, 3, 256, 1024), bf16),
            pltpu.VMEM((2, 3, ROWS, 1024), bf16),
            pltpu.VMEM((2, REACH, 1024), bf16),
            pltpu.VMEM((REACH, 1024), f32),
            pltpu.VMEM((REACH, 1024), f32),
            pltpu.VMEM((REACH, 1024), f32),
            pltpu.VMEM((KEPT, 1024), f32),
            pltpu.VMEM((3, GROUP, 1024), bf16),
            pltpu.VMEM((8, GROUP, 256), bf16),
            pltpu.VMEM((2, 4, 2, GROUP, 256), bf16),
            pltpu.VMEM((2, GROUP, 256), bf16),
            pltpu.VMEM((2, 2, GROUP, 256), bf16),
            pltpu.VMEM((N, 1024), f32),
            pltpu.VMEM((REACH, CHUNK), bf16),
            pltpu.VMEM((REACH, CHUNK), bf16),
            pltpu.VMEM((3, KEPT, CHUNK), f32),
            dma((2, 4, 2)), dma((2, 4, 2)), dma((4,)), dma((4,)), dma((9,)),
            dma((2, 5)), dma((2, 5)), dma((2, 5)), dma((8, 2)), dma((4, 2, 2)), dma((8,)), dma((4, 2)), dma((2,)),
            dma((2, 2)), dma((4,)), dma((2, 2)), dma((4,)), dma((2, 2)), dma((2, 2)),
        ],
        compiler_params=pltpu.CompilerParams(
            collective_id=0, has_side_effects=True, vmem_limit_bytes=60 * 1024 * 1024
        ),
    )(
        in_weights[0], short_taps[0], long_taps[0], first_saved[0], second_saved[0],
        first_cotangent[0], last_cotangent,
        FORWARD.astype(bf16), INVERSE.astype(bf16), FORWARD[:, :HALF],
    )
    return first[None], second[None]


def solution(mesh):
    in_specs = (
        P("section", None, "ctx", "tp"),
        P("section", None, None, "tp"),
        P("section", None, "tp"),
        P("section", None, "ctx", "tp"),
        P("section", None, "ctx", "tp"),
        P("section", "ctx", "tp"),
        P("ctx", "tp"),
    )
    out_specs = (P("section", "ctx", "tp"), P("section", "ctx", "tp"))
    return jax.shard_map(body, mesh=mesh, in_specs=in_specs, out_specs=out_specs, check_vma=False)
```

```python
import functools

import numpy as np
import jax
import jax.numpy as jnp
from jax import lax
from jax.experimental import pallas as pl
from jax.experimental.pallas import tpu as pltpu
from jax.sharding import PartitionSpec as P

MESH = pl.DeviceIdType.MESH
N = 256
HALF = 128
BEFORE = 144
AFTER = 160
GROUP = 512
ROWS = BEFORE + GROUP + AFTER
REACH = GROUP + AFTER
KEPT = GROUP + 16
CHUNK = 256
TILE = 32
FAR = 224
f32 = jnp.float32
bf16 = jnp.bfloat16


def shifted_dft():
    k = np.arange(HALF)[:, None] + 0.5
    n = np.arange(N)[None, :]
    angle = 2.0 * np.pi * k * n / N
    forward = np.concatenate([np.cos(angle), -np.sin(angle)], axis=0)
    return forward.astype(np.float32), (forward.T * (2.0 / N)).astype(np.float32)


FORWARD, INVERSE = shifted_dft()


def dot(a, b):
    return jnp.dot(a, b, preferred_element_type=f32)


def filtered(forward, inverse, signal, real, imag):
    spectrum = dot(forward, signal)
    a, b = spectrum[:HALF], spectrum[HALF:]
    mixed = jnp.concatenate([a * real - b * imag, a * imag + b * real], axis=0).astype(bf16)
    return dot(inverse, mixed)


def kernel(
    w_ref, short_ref, long_ref, u1_ref, u2_ref, g1_ref, gl_ref, fwd_ref, inv_ref, fwd32_ref,
    out1_ref, out2_ref,
    wb, ue, ge, p0, p1, p2, mx, di, pb, rb, tb, sb, resp, pr, dm, df,
    ring_s, ring_r, x_s, x_r, loc, halo_s, halo_r, pass_s, tp_s, tp_r, sum_s, sum_r, late_s, late_r, hop_r, main_s, main_r,
    edge_s, edge_r, fin_s, fin_r,
):
    s = lax.axis_index("section")
    c = lax.axis_index("ctx")
    k = lax.axis_index("tp")
    z, h = c // 2, c % 2
    up, down = (z + 1) % 8, (z + 7) % 8
    partner = 2 * z + 1 - h
    last = s == 3

    def remote(src, dst, send, recv, device):
        return pltpu.make_async_remote_copy(
            src_ref=src, dst_ref=dst, send_sem=send, recv_sem=recv,
            device_id=device, device_id_type=MESH,
        )

    barrier = pltpu.get_barrier_semaphore()

    def greet(device):
        pl.semaphore_signal(barrier, inc=1, device_id=device, device_id_type=MESH)

    greet({"ctx": partner})
    for zz in (up, down):
        for hh in range(2):
            greet({"ctx": 2 * zz + hh})
    for step in range(1, 4):
        greet({"tp": (k + step) % 4})

    @pl.when(s < 3)
    def _():
        for zz in (z, up):
            for hh in range(2):
                greet({"section": s + 1, "ctx": 2 * zz + hh})

    pl.semaphore_wait(barrier, 8 + 4 * ((s + 3) // 4))

    def ring(to_right, step, piece, rows=None):
        target = {"ctx": 2 * (up if to_right else down) + h}
        rows = rows or (128 * piece, 128)
        part = pl.ds(*rows)
        source = step if to_right else (8 - step) % 8
        dest = step + 1 if to_right else 7 - step
        src = w_ref.at[:, part] if step == 0 else wb.at[source, :, part]
        way = 0 if to_right else 1
        return remote(src, wb.at[dest, :, part], ring_s.at[way, step, piece], ring_r.at[way, step, piece], target)

    def ends(hh, piece):
        if hh == 0:
            return ring(True, 3, 0) if piece == 0 else ring(True, 3, 1, (128, FAR - 128))
        return ring(False, 3, 1) if piece == 1 else ring(False, 3, 0, (256 - FAR, FAR - 128))

    def short_end(hh):
        return ring(False, 3, 1, (FAR, 256 - FAR)) if hh == 0 else ring(True, 3, 0, (0, 256 - FAR))

    def by_column(act):
        for hh in range(2):
            pl.when(h == hh)(functools.partial(act, hh))

    def hand_on(step, turn):
        def act(hh):
            piece = turn if hh == 0 else 1 - turn
            for to_right in ((False, True) if hh == 1 else (True, False)):
                ring(to_right, step, piece).wait_recv()
                if step < 2:
                    ring(to_right, step + 1, piece).start()
                elif to_right == (hh == 0):
                    ends(hh, piece).start()
                elif turn == 1:
                    short_end(hh).start()

        by_column(act)

    def begin(hh):
        for turn in range(2):
            for to_right in (True, False):
                ring(to_right, 0, turn if hh == 0 else 1 - turn).start()

    by_column(begin)

    own_rows = pl.ds(pl.multiple_of(BEFORE + 256 * h, 16), 256)
    other_rows = pl.ds(pl.multiple_of(BEFORE + 256 * (1 - h), 16), 256)
    own_g = pl.ds(pl.multiple_of(256 * h, 256), 256)
    other_g = pl.ds(pl.multiple_of(256 * (1 - h), 256), 256)
    saved = (u1_ref, u2_ref)
    grads = (g1_ref, gl_ref)

    local_w = pltpu.make_async_copy(w_ref, wb.at[0], loc.at[0])
    local_u = [pltpu.make_async_copy(saved[i], ue.at[i, :, own_rows], loc.at[1 + i]) for i in range(2)]
    local_g = [pltpu.make_async_copy(grads[i], ge.at[i, own_g], loc.at[3 + i]) for i in range(2)]
    send_u = [
        remote(saved[i], ue.at[i, :, own_rows], x_s.at[i], x_r.at[i], {"ctx": partner}) for i in range(2)
    ]
    send_g = [
        remote(grads[i], ge.at[i, own_g], x_s.at[2 + i], x_r.at[2 + i], {"ctx": partner})
        for i in range(2)
    ]
    get_u = [
        remote(saved[i], ue.at[i, :, other_rows], x_s.at[i], x_r.at[i], {"ctx": partner}) for i in range(2)
    ]
    get_g = [
        remote(grads[i], ge.at[i, other_g], x_s.at[2 + i], x_r.at[2 + i], {"ctx": partner})
        for i in range(2)
    ]

    def before_parts(i):
        return [
            (saved[i].at[pl.ds(1, 2), pl.ds(256 - BEFORE, BEFORE)], ue.at[i, pl.ds(1, 2), pl.ds(0, BEFORE)], 0),
            (saved[i].at[0, pl.ds(240, 16)], ue.at[i, 0, pl.ds(BEFORE - 16, 16)], 1),
        ]

    def after_parts(i):
        return [
            (saved[i].at[0, pl.ds(0, AFTER)], ue.at[i, 0, pl.ds(BEFORE + GROUP, AFTER)], 2),
            (saved[i].at[pl.ds(1, 2), pl.ds(0, 32)], ue.at[i, pl.ds(1, 2), pl.ds(BEFORE + GROUP, 32)], 3),
        ]

    def grad_parts(i):
        return [(grads[i].at[pl.ds(0, AFTER)], ge.at[i, pl.ds(GROUP, AFTER)], 4)]

    def along(i, parts, to):
        return [remote(src, dst, halo_s.at[i, n], halo_r.at[i, n], {"ctx": to}) for src, dst, n in parts]

    def onward(i, parts):
        return [remote(dst, dst, pass_s.at[i, n], halo_r.at[i, n], {"ctx": partner}) for _, dst, n in parts]

    def start_halos(i, with_u, with_g):
        @pl.when(h == 1)
        def _():
            if with_u:
                for copy in along(i, before_parts(i), 2 * up + 1):
                    copy.start()

        @pl.when(h == 0)
        def _():
            for copy in along(i, after_parts(i) * with_u + grad_parts(i) * with_g, 2 * down):
                copy.start()

    def end_halos(i, with_u, with_g):
        @pl.when(h == 1)
        def _():
            if with_u:
                for copy in along(i, before_parts(i), 2 * up + 1) + onward(i, before_parts(i)):
                    copy.wait_send()

        @pl.when(h == 0)
        def _():
            parts = after_parts(i) * with_u + grad_parts(i) * with_g
            for copy in along(i, parts, 2 * down) + onward(i, parts):
                copy.wait_send()

    def pass_halos(i, with_u, with_g):
        @pl.when(h == 1)
        def _():
            if with_u:
                for copy in along(i, before_parts(i), 2 * up + 1):
                    copy.wait_recv()

                @pl.when(z == 0)
                def _():
                    ue[i, pl.ds(0, 3), pl.ds(BEFORE - 16, 16)] = jnp.zeros((3, 16, 1024), bf16)
                    ue[i, pl.ds(1, 2), pl.ds(0, BEFORE - 16)] = jnp.zeros((2, BEFORE - 16, 1024), bf16)

                for copy in onward(i, before_parts(i)):
                    copy.start()

        @pl.when(h == 0)
        def _():
            parts = after_parts(i) * with_u + grad_parts(i) * with_g
            for copy in along(i, parts, 2 * down):
                copy.wait_recv()

            if with_g:
                @pl.when(z == 7)
                def _():
                    ge[i, pl.ds(GROUP, AFTER)] = jnp.zeros((AFTER, 1024), bf16)

            for copy in onward(i, parts):
                copy.start()

    def receive_halos(i, with_u, with_g):
        @pl.when(h == 1)
        def _():
            for copy in onward(i, after_parts(i) * with_u + grad_parts(i) * with_g):
                copy.wait_recv()

        @pl.when(h == 0)
        def _():
            if with_u:
                for copy in onward(i, before_parts(i)):
                    copy.wait_recv()

    local_u[0].start()
    local_g[0].start()
    send_u[0].start()
    send_g[0].start()
    start_halos(0, True, True)
    local_w.start()
    local_u[1].start()

    @pl.when(last)
    def _():
        local_g[1].start()

    resp[...] = jnp.dot(
        fwd32_ref[...], long_ref[...], precision=lax.Precision.HIGHEST, preferred_element_type=f32
    )

    def columns(r):
        return pl.ds(pl.multiple_of(r * CHUNK, CHUNK), CHUNK)

    def features(i):
        def chunk(r, _):
            cols = columns(r)

            def short(m, x):
                total = x[16:] * short_ref[m, 0:1, cols]
                for tap in range(1, 7):
                    total += pltpu.roll(x, tap, 0)[16:] * short_ref[m, tap : tap + 1, cols]
                return total

            def tile(b, _):
                here = pl.ds(pl.multiple_of(b * TILE, TILE), TILE)
                wide = pl.ds(pl.multiple_of(b * TILE, TILE), TILE + 16)
                key = short(1, ue[i, 1, wide, cols].astype(f32))
                value = short(2, ue[i, 2, wide, cols].astype(f32))
                p1[here, cols] = key
                p2[here, cols] = value
                pr[here] = (key * value).astype(bf16)
                wide = pl.ds(pl.multiple_of(BEFORE - 16 + b * TILE, 16), TILE + 16)
                p0[here, cols] = short(0, ue[i, 0, wide, cols].astype(f32))
                return 0

            lax.fori_loop(0, REACH // TILE, tile, 0)
            real, imag = resp[:HALF, cols], resp[HALF:, cols]
            for b in range(4):
                mx[HALF * b : HALF * (b + 1), cols] = filtered(
                    fwd_ref[...], inv_ref[HALF:], pr[HALF * b : HALF * b + N], real, imag
                )
            mx[GROUP:KEPT, cols] = filtered(
                fwd_ref[:, :AFTER], inv_ref[HALF : HALF + 16], pr[GROUP:REACH], real, imag
            )
            return 0

        lax.fori_loop(0, 4, chunk, 0)

    def take_relay(r):
        cols = columns(r)

        @pl.when(s < 3)
        def _():
            remote(sb.at[0, 0], ge.at[1, pl.ds(0, GROUP), cols], main_s.at[0, 0], main_r.at[r],
                   {"ctx": partner}).wait_recv()
            remote(sb.at[0, 0, pl.ds(0, AFTER)], ge.at[1, pl.ds(GROUP, AFTER), cols], edge_s.at[0, 0],
                   edge_r.at[r], {"ctx": partner}).wait_recv()

            @pl.when(z == 7)
            def _():
                ge[1, pl.ds(GROUP, AFTER), cols] = jnp.zeros((AFTER, CHUNK), bf16)

    def gradients(i):
        def chunk(r, _):
            cols = columns(r)
            if i == 1:
                take_relay(r)

            def scale(b, _):
                here = pl.ds(pl.multiple_of(b * TILE, TILE), TILE)
                dm[here] = (ge[i, here, cols].astype(f32) * p0[here, cols]).astype(bf16)
                return 0

            lax.fori_loop(0, REACH // TILE, scale, 0)
            real, imag = resp[:HALF, cols], -resp[HALF:, cols]
            for b in range(5):
                rows = HALF if b < 4 else 16
                span = N if b < 4 else AFTER
                begin = HALF * b
                dproduct = filtered(
                    fwd_ref[:, :span], inv_ref[:rows], dm[begin : begin + span], real, imag
                )
                there = slice(begin, begin + rows)
                shifted = slice(begin + HALF, begin + HALF + rows)
                df[0, there] = ge[i, there, cols].astype(f32) * mx[there, cols]
                df[1, there] = dproduct * p2[shifted, cols]
                df[2, there] = dproduct * p1[shifted, cols]

            def tile(n, _):
                b, side = n // 2, n % 2
                here = pl.ds(pl.multiple_of(b * HALF, HALF), HALF)
                wide = pl.ds(pl.multiple_of(b * HALF, HALF), HALF + 8)
                part = pl.ds(pl.multiple_of(side * 128, 128), 128)
                there = pl.ds(pl.multiple_of(r * CHUNK + side * 128, 128), 128)
                for m in range(3):
                    x = df[m, wide, part]
                    total = x[:HALF] * short_ref[m, 0:1, there]
                    for tap in range(1, 7):
                        total += pltpu.roll(x, HALF + 8 - tap, 0)[:HALF] * short_ref[m, tap : tap + 1, there]
                    di[m, here, there] = total.astype(bf16)
                return 0

            lax.fori_loop(0, 8, tile, 0)
            return 0

        lax.fori_loop(0, 4, chunk, 0)

    def place(j):
        zt = (z + 8 - j) % 8
        return zt // 2, zt % 2

    def half_copy(j, half):
        kt, q = place(j)
        cols = pl.ds(128 * half if isinstance(half, int) else pl.multiple_of(128 * half, 128), 128)
        return remote(pb.at[j, :, cols], rb.at[0, k, q, :, cols], tp_s.at[j, half], tp_r.at[k, q, half], {"tp": kt})

    def end_first(j):
        kt, _ = place(j)

        @pl.when(kt != k)
        def _():
            for half in range(2):
                half_copy(j, half).wait_send()

    def sum_parts(j, q, src, to):
        return (
            remote(pb.at[j, other_g], rb.at[1, src, q, other_g], sum_s.at[j], sum_r.at[src, q], {"tp": to}),
            remote(pb.at[j, own_g], rb.at[1, src, q, own_g], late_s.at[q], late_r.at[q], {"tp": to}),
        )

    def end_second(j):
        kt, q = place(j)
        in_parts = kt == (k + 1 + 2 * q) % 4

        @pl.when(in_parts)
        def _():
            for copy in sum_parts(j, q, k, kt):
                copy.wait_send()

        @pl.when((kt != k) & jnp.logical_not(in_parts))
        def _():
            remote(pb.at[j], rb.at[1, k, q], sum_s.at[j], sum_r.at[k, q], {"tp": kt}).wait_send()

    def product(j):
        total = None
        for m in range(3):
            term = lax.dot_general(di[m], wb[j, m], (((1,), (1,)), ((), ())), preferred_element_type=f32)
            total = term if total is None else total + term
        return total.astype(bf16)

    def multiply_first(lo, hi):
        def unit(n, _):
            odd = n % 2
            j = odd * ((n + 1) // 2) + (1 - odd) * ((8 - n // 2) % 8)
            pb[j] = product(j)
            kt, _q = place(j)

            @pl.when(kt != k)
            def _():
                for half in range(2):
                    half_copy(j, half).start()

            return 0

        lax.fori_loop(lo, hi, unit, 0)

    def multiply_half(turn):
        half = turn * (1 - h) + (1 - turn) * h
        rows = pl.ds(pl.multiple_of(128 * half, 128), 128)
        total = None
        for m in range(3):
            term = lax.dot_general(
                di[m], wb[4, m, rows], (((1,), (1,)), ((), ())), preferred_element_type=f32
            )
            total = term if total is None else total + term
        pb[4, :, rows] = total.astype(bf16)
        kt, _ = place(4)

        @pl.when(kt != k)
        def _():
            half_copy(4, half).start()

    def multiply_second():
        def unit(n, _):
            odd, pair = n % 2, n // 2
            away = jnp.where(pair == 0, 2, jnp.where(pair == 2, 0, 1 + 2 * odd))
            q = jnp.where(pair == 1, 1 - odd, odd)
            target = (k + away) % 4
            j = (z + 8 - 2 * target - q) % 8
            end_first(j)
            pb[j] = product(j)

            @pl.when(n < 2)
            def _():
                remote(pb.at[j], tb.at[q], sum_s.at[j], hop_r.at[q], {"tp": (k + 1 + 2 * q) % 4}).start()

            @pl.when(n >= 6)
            def _():
                remote(pb.at[j], tb.at[q], sum_s.at[j], hop_r.at[q], {"tp": target}).wait_recv()
                pb[j] = (pb[j].astype(f32) + tb[q].astype(f32)).astype(bf16)

            @pl.when(pair == 3)
            def _():
                for copy in sum_parts(j, q, k, target):
                    copy.start()

            @pl.when(pair == 1)
            def _():
                remote(pb.at[j], rb.at[1, k, q], sum_s.at[j], sum_r.at[k, q], {"tp": target}).start()

            return 0

        lax.fori_loop(0, 8, unit, 0)

    def combine(i, q, rows=None):
        cols = columns(h + 2 * q)
        steps = (1, 2, 3) if i == 0 else (1, 3)
        for step in steps:
            src = (k + step) % 4
            if i == 1:
                if step == 3 - 2 * q:
                    sum_parts(0, q, src, src)[rows].wait_recv()
                elif rows == 0:
                    remote(pb.at[0], rb.at[1, src, q], sum_s.at[0], sum_r.at[src, q], {"tp": src}).wait_recv()
                continue
            for half in range(2):
                part = pl.ds(128 * half, 128)
                remote(pb.at[0, :, part], rb.at[0, src, q, :, part], tp_s.at[0, half],
                       tp_r.at[src, q, half], {"tp": src}).wait_recv()
        mine = (z + 8 - 2 * k - q) % 8

        start = 0 if i == 0 else 256 * ((1 - h) if rows == 0 else h)

        def tile(b, _):
            here = pl.ds(pl.multiple_of(start + b * 64, 64), 64)
            total = ge[i, here, cols].astype(f32) + pb[mine, here].astype(f32)
            for step in steps:
                total += rb[i, (k + step) % 4, q, here].astype(f32)
            sb[i, q, here] = total.astype(bf16)
            return 0

        lax.fori_loop(0, (GROUP if i == 0 else 256) // 64, tile, 0)

    outs = (out1_ref, out2_ref)

    def finals(i, q):
        mine, theirs = columns(h + 2 * q), columns(1 - h + 2 * q)
        keep = pltpu.make_async_copy(sb.at[i, q, own_g], outs[i].at[:, mine], loc.at[5 + 2 * i + q])
        give = remote(sb.at[i, q, other_g], outs[i].at[:, mine], fin_s.at[i, q], fin_r.at[i, q], {"ctx": partner})
        take = remote(sb.at[i, q, other_g], outs[i].at[:, theirs], fin_s.at[i, q], fin_r.at[i, q], {"ctx": partner})
        return keep, give, take

    def relay(q, hh):
        r = h + 2 * q
        to = {"section": lax.rem(s + 3, 4), "ctx": 2 * z + hh}
        edge_to = {"section": lax.rem(s + 3, 4), "ctx": 2 * down + hh}
        return (
            remote(sb.at[0, q], ge.at[1, pl.ds(0, GROUP), columns(r)], main_s.at[q, hh], main_r.at[r], to),
            remote(sb.at[0, q, pl.ds(0, AFTER)], ge.at[1, pl.ds(GROUP, AFTER), columns(r)],
                   edge_s.at[q, hh], edge_r.at[r], edge_to),
        )

    hand_on(0, 0)
    hand_on(0, 1)
    pass_halos(0, True, True)
    local_u[0].wait()
    local_g[0].wait()
    get_u[0].wait_recv()
    get_g[0].wait_recv()
    send_u[1].start()
    start_halos(1, True, False)

    @pl.when(last)
    def _():
        send_g[1].start()
        start_halos(1, False, True)

    receive_halos(0, True, True)
    hand_on(1, 0)
    features(0)
    hand_on(1, 1)
    gradients(0)
    local_w.wait()
    multiply_first(0, 5)
    pass_halos(1, True, False)

    @pl.when(last)
    def _():
        pass_halos(1, False, True)

    hand_on(2, 0)
    local_u[1].wait()
    get_u[1].wait_recv()
    receive_halos(1, True, False)
    features(1)
    hand_on(2, 1)

    @pl.when(last)
    def _():
        local_g[1].wait()
        get_g[1].wait_recv()
        receive_halos(1, False, True)

    multiply_first(5, 7)
    by_column(lambda hh: ends(hh, hh).wait_recv())
    multiply_half(0)

    def arrive(hh):
        ends(hh, 1 - hh).wait_recv()
        short_end(hh).wait_recv()

    by_column(arrive)
    multiply_half(1)
    for q in range(2):
        combine(0, q)

        @pl.when(s > 0)
        def _():
            for copy in relay(q, 0) + relay(q, 1):
                copy.start()

    gradients(1)
    for q in range(2):
        keep, give, _ = finals(0, q)
        keep.start()
        give.start()
    multiply_second()
    for q in range(2):
        combine(1, q, 0)
        finals(1, q)[1].start()
    for q in range(2):
        combine(1, q, 1)
        finals(1, q)[0].start()

    def sent(hh):
        for to_right in (True, False):
            for step in range(3):
                for piece in range(2):
                    ring(to_right, step, piece).wait_send()
        for copy in (ends(hh, 0), ends(hh, 1), short_end(hh)):
            copy.wait_send()

    by_column(sent)
    for i in range(2):
        send_u[i].wait_send()
        end_halos(i, True, i == 0)
    send_g[0].wait_send()

    @pl.when(last)
    def _():
        send_g[1].wait_send()
        end_halos(1, False, True)

    @pl.when(s > 0)
    def _():
        for q in range(2):
            for copy in relay(q, 0) + relay(q, 1):
                copy.wait_send()

    def finish(j, _):
        end_second(j)
        return 0

    lax.fori_loop(0, 8, finish, 0)
    for i in range(2):
        for q in range(2):
            keep, give, take = finals(i, q)
            keep.wait()
            give.wait_send()
            take.wait_recv()


def body(
    in_weights, short_taps, long_taps, first_saved, second_saved, first_cotangent, last_cotangent
):
    anywhere = pl.BlockSpec(memory_space=pl.ANY)
    vmem = pl.BlockSpec(memory_space=pltpu.VMEM)
    dma = pltpu.SemaphoreType.DMA
    first, second = pl.pallas_call(
        kernel,
        out_shape=(jax.ShapeDtypeStruct((256, 1024), bf16),) * 2,
        in_specs=[anywhere, vmem, vmem, anywhere, anywhere, anywhere, anywhere, vmem, vmem, vmem],
        out_specs=(anywhere, anywhere),
        scratch_shapes=[
            pltpu.VMEM((8, 3, 256, 1024), bf16),
            pltpu.VMEM((2, 3, ROWS, 1024), bf16),
            pltpu.VMEM((2, REACH, 1024), bf16),
            pltpu.VMEM((REACH, 1024), f32),
            pltpu.VMEM((REACH, 1024), f32),
            pltpu.VMEM((REACH, 1024), f32),
            pltpu.VMEM((KEPT, 1024), f32),
            pltpu.VMEM((3, GROUP, 1024), bf16),
            pltpu.VMEM((8, GROUP, 256), bf16),
            pltpu.VMEM((2, 4, 2, GROUP, 256), bf16),
            pltpu.VMEM((2, GROUP, 256), bf16),
            pltpu.VMEM((2, 2, GROUP, 256), bf16),
            pltpu.VMEM((N, 1024), f32),
            pltpu.VMEM((REACH, CHUNK), bf16),
            pltpu.VMEM((REACH, CHUNK), bf16),
            pltpu.VMEM((3, KEPT, CHUNK), f32),
            dma((2, 4, 2)), dma((2, 4, 2)), dma((4,)), dma((4,)), dma((9,)),
            dma((2, 5)), dma((2, 5)), dma((2, 5)), dma((8, 2)), dma((4, 2, 2)), dma((8,)), dma((4, 2)), dma((2,)), dma((2,)), dma((2,)),
            dma((2, 2)), dma((4,)), dma((2, 2)), dma((4,)), dma((2, 2)), dma((2, 2)),
        ],
        compiler_params=pltpu.CompilerParams(
            collective_id=0, has_side_effects=True, vmem_limit_bytes=60 * 1024 * 1024
        ),
    )(
        in_weights[0], short_taps[0], long_taps[0], first_saved[0], second_saved[0],
        first_cotangent[0], last_cotangent,
        FORWARD.astype(bf16), INVERSE.astype(bf16), FORWARD[:, :HALF],
    )
    return first[None], second[None]


def solution(mesh):
    in_specs = (
        P("section", None, "ctx", "tp"),
        P("section", None, None, "tp"),
        P("section", None, "tp"),
        P("section", None, "ctx", "tp"),
        P("section", None, "ctx", "tp"),
        P("section", "ctx", "tp"),
        P("ctx", "tp"),
    )
    out_specs = (P("section", "ctx", "tp"), P("section", "ctx", "tp"))
    return jax.shard_map(body, mesh=mesh, in_specs=in_specs, out_specs=out_specs, check_vma=False)
```
